512 devices in a mesh: row: 8 (over y), col: 64 (over x, z, core).
Axes of the slice: x: 4, y: 8, z: 8, core: 2. Of those that a mesh axis runs over, the one named last changes fastest.
Arguments:
- integrals: float32 [2, 16384, 16384], P(None, 'row', 'col'), may hold values from -6 to 6
- coefs: float32 [16384, 1024], P('row', 'col'), may hold values from -0.125 to 0.125
- screen: int32 [128, 128], P('row', 'col'), may hold values from 0 to 1
- domains: int32 [8, 80], replicated, may hold values from 0 to 127, as said below
Outputs:
- pair_ints: float32 [2, 1024, 1024], P(None, 'row', 'col')
The draws below stay inside these ranges and needn't reach their ends.
Inputs may be any that keep to these rules, and one draw needn't show every extreme that they name: `domains`: each row lists 80 distinct basis tiles, consecutive modulo 128.
All inputs are finite; a program needn't handle non-finite values.
Results may differ from the reference program's by a relative error of at most 0.000098.
Values sent between devices are 32-bit elements; how exact they have to be, the bound alone decides.
No kernel may reach another device: no remote copies, remote signals or barrier semaphores. Data moves between devices by JAX's collectives and lax.ppermute only.
A program may use at most 128 MiB of HBM per device.

```python
import jax
import jax.numpy as jnp
from jax import lax

TILE = 128
NBF = 16384
NOCC = 1024
NAUX = 2
NBT = 128
OT = 8
DOM = 80


def draw_screen(key, part):
    key = jax.random.fold_in(key, 11)
    tile_ids = jnp.arange(NBT, dtype=jnp.int32)
    distance = jnp.abs(tile_ids[:, None] - tile_ids[None, :])
    near = distance < NBT // 6
    tail = jax.random.randint(key, (NBT, NBT), 0, 10) < 1
    return jnp.where(near | tail, 1, 0).astype(jnp.int32)


def draw_domains(key, part):
    key = jax.random.fold_in(key, 7)
    spacing = NBT // OT
    jitter = jax.random.randint(key, (OT,), 0, spacing)
    starts = jnp.arange(OT, dtype=jnp.int32) * spacing + jitter
    offsets = jnp.arange(DOM, dtype=jnp.int32)
    chosen = (starts[:, None] + offsets[None, :]) % NBT
    return chosen.astype(jnp.int32)


def levels(own_key, dims, split, least, top_value):
    def one(position, blocks):
        draws = jax.random.uniform(jax.random.fold_in(jax.random.fold_in(own_key, 6), position), (blocks,), jnp.float32, least / len(split), top_value / len(split))
        return jnp.repeat(jnp.exp(draws), dims[position] // blocks).reshape((-1,) + (1,) * (len(dims) - position - 1))

    gain = one(*split[0])
    for cut in split[1:]:
        gain = gain * one(*cut)
    return gain


def gaussian(own_key, extent, scale, most, cuts=(), kind=jnp.bfloat16):
    values = scale * jax.random.normal(own_key, extent, jnp.float32)
    if cuts:
        values = values * levels(own_key, extent, cuts, -0.22, 0.18)
    return jnp.clip(values, -most, most).astype(kind)


def setup_inputs(seed: int = 0) -> dict:
    key_of = jax.random.split(jax.random.key(seed), 5)
    integrals = gaussian(key_of[0], (NAUX, NBF, NBF), 1.0, 6.0, ((1, 8), (2, 64)), jnp.float32)
    coefs = gaussian(key_of[1], (NBF, NOCC), (3 * NBF // 20) ** -0.5, 0.125, ((0, 8), (1, 64)), jnp.float32)
    screen = draw_screen(jax.random.fold_in(key_of[4], 71), 0)
    domains = draw_domains(jax.random.fold_in(key_of[4], 71), 0)
    return dict(integrals=integrals, coefs=coefs, screen=screen, domains=domains)


def domain_table(domains):
    tile_ids = jnp.arange(NBT, dtype=jnp.int32)
    in_domain = jnp.any(domains[None, :, :] == tile_ids[:, None, None], axis=2)
    return in_domain.astype(jnp.float32)


def reference(integrals, coefs, screen, domains):
    domain_hits = domain_table(domains)
    coef_eff = (coefs.reshape(NBT, TILE, OT, TILE) * domain_hits[:, None, :, None]).reshape(NBF, NOCC)
    pair_keep = screen.astype(jnp.float32)

    def transform_slab(aux_slab):
        screened = (aux_slab.reshape(NBT, TILE, NBT, TILE) * pair_keep[:, None, :, None]).reshape(NBF, NBF)
        half_sum = jnp.dot(coef_eff.T, screened, precision=lax.Precision.HIGHEST, preferred_element_type=jnp.float32)
        return jnp.dot(half_sum, coef_eff, precision=lax.Precision.HIGHEST, preferred_element_type=jnp.float32)

    return lax.map(transform_slab, integrals)
```

```python
import jax
import jax.numpy as jnp
from jax import lax
from jax.experimental import pallas as pl
from jax.experimental.pallas import tpu as pltpu
from jax.sharding import Mesh, PartitionSpec as P

TILE = 128
NX, NZ = 4, 8
BF16 = jnp.bfloat16
F32 = jnp.float32


def split(value):
    high = value.astype(BF16)
    return high, (value - high.astype(F32)).astype(BF16)


def swap(value):
    return lax.ppermute(value, "core", [(0, 1), (1, 0)])


def gather(value, axis):
    copies = jnp.broadcast_to(value[None], (lax.axis_size(axis),) + value.shape)
    return lax.all_to_all(copies, axis, 0, 0, tiled=True)


def pieces_kernel(core_ref, own_ref, other_ref, high_ref, low_ref):
    first = core_ref[0] == 0
    own, other = own_ref[0], other_ref[0]
    width = own.shape[1]
    for place, value in enumerate((jnp.where(first, own, other), jnp.where(first, other, own))):
        high, low = split(value)
        high_ref[:, place * width : (place + 1) * width] = high
        low_ref[:, place * width : (place + 1) * width] = low


def pieces(core, own, other):
    aux, rows, width = own.shape
    step = 512
    block = pl.BlockSpec((1, step, width), lambda p, m, core: (p, m, 0))
    out = pl.BlockSpec((step, 2 * width), lambda p, m, core: (m, p))
    shape = jax.ShapeDtypeStruct((rows, aux * 2 * width), BF16)
    return pl.pallas_call(
        pieces_kernel,
        out_shape=(shape, shape),
        grid_spec=pltpu.PrefetchScalarGridSpec(
            num_scalar_prefetch=1,
            grid=(aux, rows // step),
            in_specs=[block, block],
            out_specs=(out, out),
        ),
        compiler_params=pltpu.CompilerParams(vmem_limit_bytes=32 * 2**20),
    )(core, own, other)


def first_kernel(coef_ref, high_ref, low_ref, out_ref, coef_high, coef_low):
    @pl.when(pl.program_id(0) == 0)
    def _():
        high, low = split(coef_ref[...])
        coef_high[...] = high
        coef_low[...] = low

    total = jnp.dot(coef_high[...], low_ref[...], preferred_element_type=F32)
    total += jnp.dot(coef_low[...], high_ref[...], preferred_element_type=F32)
    total += jnp.dot(coef_high[...], high_ref[...], preferred_element_type=F32)
    for z in range(NZ):
        for x in range(NX):
            start = (z * NX + x) * 16
            out_ref[x, z // 4, z % 4] = total[start : start + 16]


def first(coef, high, low):
    occ, depth = coef.shape
    width = high.shape[1]
    step = 256
    piece = pl.BlockSpec((depth, step), lambda n: (0, n))
    return pl.pallas_call(
        first_kernel,
        out_shape=jax.ShapeDtypeStruct((NX, 2, 4, 16, width), F32),
        grid=(width // step,),
        in_specs=[pl.BlockSpec((occ, depth), lambda n: (0, 0)), piece, piece],
        out_specs=pl.BlockSpec((NX, 2, 4, 16, step), lambda n: (0, 0, 0, 0, n)),
        scratch_shapes=[pltpu.VMEM((occ, depth), BF16), pltpu.VMEM((occ, depth), BF16)],
        compiler_params=pltpu.CompilerParams(vmem_limit_bytes=56 * 2**20),
        cost_estimate=pl.CostEstimate(
            flops=6 * occ * depth * width, bytes_accessed=14 * 2**20, transcendentals=0
        ),
    )(coef, high, low)


def second_kernel(rows_ref, half_ref, out_ref):
    half = half_ref[...]
    width = half.shape[1] // 2
    half = jnp.concatenate([half[:, :width], half[:, width:]], axis=0)
    half_high, half_low = split(half)
    rows_high, rows_low = split(rows_ref[...])

    def dot(a, b):
        return lax.dot_general(a, b, (((1,), (1,)), ((), ())), preferred_element_type=F32)

    out_ref[...] = (dot(rows_high, half_low) + dot(rows_low, half_high)) + dot(rows_high, half_high)


def second(rows, half):
    occ = rows.shape[0]
    return pl.pallas_call(
        second_kernel,
        out_shape=jax.ShapeDtypeStruct((occ, 2 * half.shape[0]), F32),
        compiler_params=pltpu.CompilerParams(vmem_limit_bytes=32 * 2**20),
    )(rows, half)


def shards(integrals, coefs, screen, domains):
    aux, row_len, col_len = integrals.shape
    occ = coefs.shape[1]
    row, core = lax.axis_index("y"), lax.axis_index("core")
    col = lax.axis_index(("x", "z", "core"))
    row_tiles = row_len // TILE

    tile_ids = row * row_tiles + jnp.arange(row_tiles, dtype=jnp.int32)
    listed = lax.dynamic_index_in_dim(domains, col * occ // TILE, 0, keepdims=False)
    in_domain = jnp.any(listed[None, :] == tile_ids[:, None], axis=1).astype(F32)
    coef = coefs.T * jnp.repeat(in_domain, TILE)[None, :]

    along_x = gather(coef, "x").reshape(NX * occ, row_len)
    gathered = lax.all_gather(along_x, "z", axis=0, tiled=True)

    keep = screen.astype(F32)
    screened = (
        integrals.reshape(aux, row_tiles, TILE, col_len // TILE, TILE) * keep[None, :, None, :, None]
    ).reshape(integrals.shape)
    high, low = pieces(core[None], screened, swap(screened))

    chip_len = 2 * col_len
    part = lax.all_to_all(coef.reshape(8, occ // 8, row_len), "y", 0, 0, tiled=True)
    part = part.reshape(8, occ // 8, row_len // chip_len, chip_len).transpose(0, 2, 1, 3)
    part = part.reshape(NX * NZ, occ // 8, chip_len)
    part = lax.all_to_all(part, ("x", "z"), 0, 0, tiled=True)
    part = gather(part, "y")
    both = jnp.stack([part, swap(part)])
    both = jnp.where(core == 0, both, both[::-1])
    rows = both.transpose(2, 0, 1, 3, 4).reshape(NX * NZ * 2 * occ, chip_len)

    half = first(gathered, high, low).reshape(NX * NZ * occ, 2 * aux * col_len)
    half = lax.psum_scatter(half, "y", scatter_dimension=0, tiled=True)
    pairs = second(rows, half)
    pairs = pairs.reshape(NX * NZ * 2, occ, pairs.shape[1])
    pairs = lax.all_to_all(pairs, ("x", "z", "core"), 0, 0, tiled=True)
    pairs = pairs.reshape(NX * NZ, 2, occ, aux, 4, occ).sum(axis=0)
    return pairs.transpose(2, 3, 0, 4, 1).reshape(aux, 8 * occ, occ)


def solution(mesh):
    devices = mesh.devices.reshape(8, NX, NZ, 2)
    split_mesh = Mesh(devices, ("y", "x", "z", "core"))
    col = ("x", "z", "core")
    placed = (P(None, "y", col), P("y", col), P("y", col), P())
    return jax.shard_map(
        shards, mesh=split_mesh, in_specs=placed, out_specs=P(None, "y", col), check_vma=False
    )
```

```python
import jax
import jax.numpy as jnp
from jax import lax
from jax.experimental import pallas as pl
from jax.experimental.pallas import tpu as pltpu
from jax.sharding import Mesh, PartitionSpec as P

TILE = 128
NX, NZ = 4, 8
BF16 = jnp.bfloat16
F32 = jnp.float32


def split(value):
    high = value.astype(BF16)
    return high, (value - high.astype(F32)).astype(BF16)


def swap(value):
    return lax.ppermute(value, "core", [(0, 1), (1, 0)])


def gather(value, axis):
    copies = jnp.broadcast_to(value[None], (lax.axis_size(axis),) + value.shape)
    return lax.all_to_all(copies, axis, 0, 0, tiled=True)


def pieces_kernel(core_ref, own_ref, other_ref, high_ref, low_ref):
    first = core_ref[0] == 0
    own, other = own_ref[0], other_ref[0]
    width = own.shape[1]
    for place, value in enumerate((jnp.where(first, own, other), jnp.where(first, other, own))):
        high, low = split(value)
        high_ref[:, place * width : (place + 1) * width] = high
        low_ref[:, place * width : (place + 1) * width] = low


def pieces(core, own, other):
    aux, rows, width = own.shape
    step = 512
    block = pl.BlockSpec((1, step, width), lambda p, m, core: (p, m, 0))
    out = pl.BlockSpec((step, 2 * width), lambda p, m, core: (m, p))
    shape = jax.ShapeDtypeStruct((rows, aux * 2 * width), BF16)
    return pl.pallas_call(
        pieces_kernel,
        out_shape=(shape, shape),
        grid_spec=pltpu.PrefetchScalarGridSpec(
            num_scalar_prefetch=1,
            grid=(aux, rows // step),
            in_specs=[block, block],
            out_specs=(out, out),
        ),
        compiler_params=pltpu.CompilerParams(vmem_limit_bytes=32 * 2**20),
    )(core, own, other)


def first_kernel(coef_ref, high_ref, low_ref, after_ref, out_ref, coef_high, coef_low):
    del after_ref
    @pl.when(pl.program_id(0) == 0)
    def _():
        high, low = split(coef_ref[...])
        coef_high[...] = high
        coef_low[...] = low

    total = jnp.dot(coef_high[...], low_ref[...], preferred_element_type=F32)
    total += jnp.dot(coef_low[...], high_ref[...], preferred_element_type=F32)
    total += jnp.dot(coef_high[...], high_ref[...], preferred_element_type=F32)
    for z in range(NZ):
        for x in range(NX):
            start = (z * NX + x) * 16
            out_ref[x, z // 4, z % 4] = total[start : start + 16]


def first(coef, high, low, after):
    occ, depth = coef.shape
    width = high.shape[1]
    step = 256
    piece = pl.BlockSpec((depth, step), lambda n: (0, n))
    return pl.pallas_call(
        first_kernel,
        out_shape=jax.ShapeDtypeStruct((NX, 2, 4, 16, width), F32),
        grid=(width // step,),
        in_specs=[
            pl.BlockSpec((occ, depth), lambda n: (0, 0)),
            piece,
            piece,
            pl.BlockSpec(memory_space=pl.ANY),
        ],
        out_specs=pl.BlockSpec((NX, 2, 4, 16, step), lambda n: (0, 0, 0, 0, n)),
        scratch_shapes=[pltpu.VMEM((occ, depth), BF16), pltpu.VMEM((occ, depth), BF16)],
        compiler_params=pltpu.CompilerParams(vmem_limit_bytes=56 * 2**20),
        cost_estimate=pl.CostEstimate(
            flops=6 * occ * depth * width, bytes_accessed=14 * 2**20, transcendentals=0
        ),
    )(coef, high, low, after)


def second_kernel(rows_ref, half_ref, out_ref):
    half = half_ref[...]
    width = half.shape[1] // 2
    half = jnp.concatenate([half[:, :width], half[:, width:]], axis=0)
    half_high, half_low = split(half)
    rows_high, rows_low = split(rows_ref[...])

    def dot(a, b):
        return lax.dot_general(a, b, (((1,), (1,)), ((), ())), preferred_element_type=F32)

    out_ref[...] = (dot(rows_high, half_low) + dot(rows_low, half_high)) + dot(rows_high, half_high)


def second(rows, half):
    occ = rows.shape[0]
    return pl.pallas_call(
        second_kernel,
        out_shape=jax.ShapeDtypeStruct((occ, 2 * half.shape[0]), F32),
        compiler_params=pltpu.CompilerParams(vmem_limit_bytes=32 * 2**20),
    )(rows, half)


def last_kernel(parts_ref, out_ref):
    count = parts_ref.shape[0] // 2
    sums = [parts_ref[core] for core in range(2)]
    for place in range(1, count):
        for core in range(2):
            sums[core] += parts_ref[2 * place + core]
    for aux in range(2):
        runs = [sums[core][:, aux * 64 + z * 16 :][:, :16] for z in range(4) for core in range(2)]
        out_ref[aux] = jnp.concatenate(runs, axis=1)


def last(parts):
    return pl.pallas_call(
        last_kernel,
        out_shape=jax.ShapeDtypeStruct((2, parts.shape[1], parts.shape[2]), F32),
    )(parts)


def shards(integrals, coefs, screen, domains):
    aux, row_len, col_len = integrals.shape
    occ = coefs.shape[1]
    row, core = lax.axis_index("y"), lax.axis_index("core")
    col = lax.axis_index(("x", "z", "core"))
    row_tiles = row_len // TILE

    tile_ids = row * row_tiles + jnp.arange(row_tiles, dtype=jnp.int32)
    listed = lax.dynamic_index_in_dim(domains, col * occ // TILE, 0, keepdims=False)
    in_domain = jnp.any(listed[None, :] == tile_ids[:, None], axis=1).astype(F32)
    coef = coefs.T * jnp.repeat(in_domain, TILE)[None, :]

    along_x = gather(coef, "x").reshape(NX * occ, row_len)
    gathered = lax.all_gather(along_x, "z", axis=0, tiled=True)

    keep = screen.astype(F32)
    screened = (
        integrals.reshape(aux, row_tiles, TILE, col_len // TILE, TILE) * keep[None, :, None, :, None]
    ).reshape(integrals.shape)
    high, low = pieces(core[None], screened, swap(screened))

    chip_len = 2 * col_len
    part = lax.all_to_all(coef.reshape(8, occ // 8, row_len), "y", 0, 0, tiled=True)
    part = part.reshape(8, occ // 8, row_len // chip_len, chip_len).transpose(0, 2, 1, 3)
    part = part.reshape(NX * NZ, occ // 8, chip_len)
    part = lax.all_to_all(part, ("x", "z"), 0, 0, tiled=True)
    occ_part = occ // 8
    part = part.reshape(NX * NZ * occ_part, chip_len)
    mine = lax.all_gather(part, "y", axis=0, tiled=True)
    both = jnp.stack([mine, swap(mine)])
    both = jnp.where(core == 0, both, both[::-1])
    rows = both.reshape(2, 8, NX * NZ, occ_part, chip_len).transpose(2, 0, 1, 3, 4)
    rows = rows.reshape(NX * NZ * 2 * occ, chip_len)

    half = first(gathered, high, low, part).reshape(NX * NZ * occ, 2 * aux * col_len)
    half = lax.psum_scatter(half, "y", scatter_dimension=0, tiled=True)
    pairs = second(rows, half)
    pairs = pairs.reshape(NX * NZ * 2, occ, pairs.shape[1])
    pairs = lax.all_to_all(pairs, ("x", "z", "core"), 0, 0, tiled=True)
    return last(pairs).transpose(0, 2, 1)


def solution(mesh):
    devices = mesh.devices.reshape(8, NX, NZ, 2)
    split_mesh = Mesh(devices, ("y", "x", "z", "core"))
    col = ("x", "z", "core")
    placed = (P(None, "y", col), P("y", col), P("y", col), P())
    return jax.shard_map(
        shards, mesh=split_mesh, in_specs=placed, out_specs=P(None, "y", col), check_vma=False
    )
```

```python
import jax
import jax.numpy as jnp
from jax import lax
from jax.experimental import pallas as pl
from jax.experimental.pallas import tpu as pltpu
from jax.sharding import Mesh, PartitionSpec as P

TILE = 128
NX, NZ = 4, 8
BF16 = jnp.bfloat16
F32 = jnp.float32


def split(value):
    high = value.astype(BF16)
    return high, (value - high.astype(F32)).astype(BF16)


def swap(value):
    return lax.ppermute(value, "core", [(0, 1), (1, 0)])


def gather(value, axis):
    copies = jnp.broadcast_to(value[None], (lax.axis_size(axis),) + value.shape)
    return lax.all_to_all(copies, axis, 0, 0, tiled=True)


def around(value, axis):
    count = lax.axis_size(axis)
    found = [value] * count
    for step in range(1, count // 2 + 1):
        found[step] = lax.ppermute(found[step - 1], axis, [(i, (i - 1) % count) for i in range(count)])
        if 2 * step < count:
            back = found[(1 - step) % count]
            found[-step] = lax.ppermute(back, axis, [(i, (i + 1) % count) for i in range(count)])
    return found


def assemble_kernel(place_ref, own_ref, other_ref, out_ref):
    row, core = place_ref[0], place_ref[1]
    count, length, _ = own_ref.shape
    places = length // 2
    for source, ref in enumerate((own_ref, other_ref)):
        which = core if source == 0 else 1 - core
        for step in range(count):
            line = lax.rem(row + step, count)
            for pair in range(2):
                start = which * 2 * count + line * 2 + pair
                out_ref[pl.ds(start, places, stride=4 * count), :] = ref[step, pl.ds(pair, places, stride=2), :]


def assemble(place, own, other):
    count, length, width = own.shape
    block = pl.BlockSpec((count, length, TILE), lambda n, place: (0, 0, n))
    return pl.pallas_call(
        assemble_kernel,
        out_shape=jax.ShapeDtypeStruct((2 * count * length, width), F32),
        grid_spec=pltpu.PrefetchScalarGridSpec(
            num_scalar_prefetch=1,
            grid=(width // TILE,),
            in_specs=[block, block],
            out_specs=pl.BlockSpec((2 * count * length, TILE), lambda n, place: (0, n)),
        ),
        compiler_params=pltpu.CompilerParams(vmem_limit_bytes=32 * 2**20),
    )(place, own, other)


def pieces_kernel(core_ref, own_ref, other_ref, high_ref, low_ref):
    first = core_ref[0] == 0
    own, other = own_ref[0], other_ref[0]
    width = own.shape[1]
    for place, value in enumerate((jnp.where(first, own, other), jnp.where(first, other, own))):
        high, low = split(value)
        high_ref[:, place * width : (place + 1) * width] = high
        low_ref[:, place * width : (place + 1) * width] = low


def pieces(core, own, other):
    aux, rows, width = own.shape
    step = 512
    block = pl.BlockSpec((1, step, width), lambda p, m, core: (p, m, 0))
    out = pl.BlockSpec((step, 2 * width), lambda p, m, core: (m, p))
    shape = jax.ShapeDtypeStruct((rows, aux * 2 * width), BF16)
    return pl.pallas_call(
        pieces_kernel,
        out_shape=(shape, shape),
        grid_spec=pltpu.PrefetchScalarGridSpec(
            num_scalar_prefetch=1,
            grid=(aux, rows // step),
            in_specs=[block, block],
            out_specs=(out, out),
        ),
        compiler_params=pltpu.CompilerParams(vmem_limit_bytes=32 * 2**20),
    )(core, own, other)


def first_kernel(coef_ref, high_ref, low_ref, after_ref, out_ref, coef_high, coef_low):
    del after_ref
    @pl.when(pl.program_id(0) == 0)
    def _():
        high, low = split(coef_ref[...])
        coef_high[...] = high
        coef_low[...] = low

    total = jnp.dot(coef_high[...], low_ref[...], preferred_element_type=F32)
    total += jnp.dot(coef_low[...], high_ref[...], preferred_element_type=F32)
    total += jnp.dot(coef_high[...], high_ref[...], preferred_element_type=F32)
    for z in range(NZ):
        for x in range(NX):
            start = (z * NX + x) * 16
            out_ref[x, z // 4, z % 4] = total[start : start + 16]


def first(coef, high, low, after):
    occ, depth = coef.shape
    width = high.shape[1]
    step = 256
    piece = pl.BlockSpec((depth, step), lambda n: (0, n))
    return pl.pallas_call(
        first_kernel,
        out_shape=jax.ShapeDtypeStruct((NX, 2, 4, 16, width), F32),
        grid=(width // step,),
        in_specs=[
            pl.BlockSpec((occ, depth), lambda n: (0, 0)),
            piece,
            piece,
            pl.BlockSpec(memory_space=pl.ANY),
        ],
        out_specs=pl.BlockSpec((NX, 2, 4, 16, step), lambda n: (0, 0, 0, 0, n)),
        scratch_shapes=[pltpu.VMEM((occ, depth), BF16), pltpu.VMEM((occ, depth), BF16)],
        compiler_params=pltpu.CompilerParams(vmem_limit_bytes=56 * 2**20),
        cost_estimate=pl.CostEstimate(
            flops=6 * occ * depth * width, bytes_accessed=14 * 2**20, transcendentals=0
        ),
    )(coef, high, low, after)


def second_kernel(rows_ref, half_ref, out_ref):
    half = half_ref[...]
    width = half.shape[1] // 2
    half = jnp.concatenate([half[:, :width], half[:, width:]], axis=0)
    half_high, half_low = split(half)
    rows_high, rows_low = split(rows_ref[...])

    def dot(a, b):
        return lax.dot_general(a, b, (((1,), (1,)), ((), ())), preferred_element_type=F32)

    out_ref[...] = (dot(rows_high, half_low) + dot(rows_low, half_high)) + dot(rows_high, half_high)


def second(rows, half):
    occ = rows.shape[0]
    return pl.pallas_call(
        second_kernel,
        out_shape=jax.ShapeDtypeStruct((occ, 2 * half.shape[0]), F32),
        compiler_params=pltpu.CompilerParams(vmem_limit_bytes=32 * 2**20),
    )(rows, half)


def last_kernel(parts_ref, out_ref):
    count = parts_ref.shape[0] // 2
    sums = [parts_ref[core] for core in range(2)]
    for place in range(1, count):
        for core in range(2):
            sums[core] += parts_ref[2 * place + core]
    for aux in range(2):
        runs = [sums[core][:, aux * 64 + z * 16 :][:, :16] for z in range(4) for core in range(2)]
        out_ref[aux] = jnp.concatenate(runs, axis=1)


def last(parts):
    return pl.pallas_call(
        last_kernel,
        out_shape=jax.ShapeDtypeStruct((2, parts.shape[1], parts.shape[2]), F32),
    )(parts)


def shards(integrals, coefs, screen, domains):
    aux, row_len, col_len = integrals.shape
    occ = coefs.shape[1]
    row, core = lax.axis_index("y"), lax.axis_index("core")
    col = lax.axis_index(("x", "z", "core"))
    row_tiles = row_len // TILE

    tile_ids = row * row_tiles + jnp.arange(row_tiles, dtype=jnp.int32)
    listed = lax.dynamic_index_in_dim(domains, col * occ // TILE, 0, keepdims=False)
    in_domain = jnp.any(listed[None, :] == tile_ids[:, None], axis=1).astype(F32)
    coef = coefs.T * jnp.repeat(in_domain, TILE)[None, :]

    along_x = gather(coef, "x").reshape(NX * occ, row_len)
    gathered = lax.all_gather(along_x, "z", axis=0, tiled=True)

    keep = screen.astype(F32)
    screened = (
        integrals.reshape(aux, row_tiles, TILE, col_len // TILE, TILE) * keep[None, :, None, :, None]
    ).reshape(integrals.shape)
    high, low = pieces(core[None], screened, swap(screened))

    chip_len = 2 * col_len
    part = lax.all_to_all(coef.reshape(8, occ // 8, row_len), "y", 0, 0, tiled=True)
    part = part.reshape(8, occ // 8, row_len // chip_len, chip_len).transpose(0, 2, 1, 3)
    part = part.reshape(NX * NZ, occ // 8, chip_len)
    part = lax.all_to_all(part, ("x", "z"), 0, 0, tiled=True)
    occ_part = occ // 8
    part = part.reshape(NX * NZ * occ_part, chip_len)
    ring = jnp.stack(around(part, "y"))
    rows = assemble(jnp.stack([row, core]), ring, swap(ring))

    half = first(gathered, high, low, part).reshape(NX * NZ * occ, 2 * aux * col_len)
    half = lax.psum_scatter(half, "y", scatter_dimension=0, tiled=True)
    pairs = second(rows, half)
    pairs = pairs.reshape(NX * NZ * 2, occ, pairs.shape[1])
    pairs = lax.all_to_all(pairs, ("x", "z", "core"), 0, 0, tiled=True)
    return last(pairs).transpose(0, 2, 1)


def solution(mesh):
    devices = mesh.devices.reshape(8, NX, NZ, 2)
    split_mesh = Mesh(devices, ("y", "x", "z", "core"))
    col = ("x", "z", "core")
    placed = (P(None, "y", col), P("y", col), P("y", col), P())
    return jax.shard_map(
        shards, mesh=split_mesh, in_specs=placed, out_specs=P(None, "y", col), check_vma=False
    )
```

```python
import jax
import jax.numpy as jnp
from jax import lax
from jax.experimental import pallas as pl
from jax.experimental.pallas import tpu as pltpu
from jax.sharding import Mesh, PartitionSpec as P

TILE = 128
NX, NZ = 4, 8
BF16 = jnp.bfloat16
F32 = jnp.float32


def split(value):
    high = value.astype(BF16)
    return high, (value - high.astype(F32)).astype(BF16)


def swap(value):
    return lax.ppermute(value, "core", [(0, 1), (1, 0)])


def gather(value, axis):
    copies = jnp.broadcast_to(value[None], (lax.axis_size(axis),) + value.shape)
    return lax.all_to_all(copies, axis, 0, 0, tiled=True)


def pieces_kernel(core_ref, own_ref, other_ref, high_ref, low_ref):
    first = core_ref[0] == 0
    own, other = own_ref[0], other_ref[0]
    width = own.shape[1]
    for place, value in enumerate((jnp.where(first, own, other), jnp.where(first, other, own))):
        high, low = split(value)
        high_ref[:, place * width : (place + 1) * width] = high
        low_ref[:, place * width : (place + 1) * width] = low


def pieces(core, own, other):
    aux, rows, width = own.shape
    step = 512
    block = pl.BlockSpec((1, step, width), lambda p, m, core: (p, m, 0))
    out = pl.BlockSpec((step, 2 * width), lambda p, m, core: (m, p))
    shape = jax.ShapeDtypeStruct((rows, aux * 2 * width), BF16)
    return pl.pallas_call(
        pieces_kernel,
        out_shape=(shape, shape),
        grid_spec=pltpu.PrefetchScalarGridSpec(
            num_scalar_prefetch=1,
            grid=(aux, rows // step),
            in_specs=[block, block],
            out_specs=(out, out),
        ),
        compiler_params=pltpu.CompilerParams(vmem_limit_bytes=56 * 2**20),
    )(core, own, other)


def first_kernel(coef_ref, high_ref, low_ref, passed_ref, out_ref, passed_out_ref, total):
    del passed_ref, passed_out_ref
    step = pl.program_id(0)
    coef_high, coef_low = split(coef_ref[...])
    part = jnp.dot(coef_high, low_ref[...], preferred_element_type=F32)
    part += jnp.dot(coef_low, high_ref[...], preferred_element_type=F32)
    part += jnp.dot(coef_high, high_ref[...], preferred_element_type=F32)

    @pl.when(step == 0)
    def _():
        total[...] = part

    @pl.when(step > 0)
    def _():
        total[...] += part

    @pl.when(step == pl.num_programs(0) - 1)
    def _():
        for z in range(NZ):
            for x in range(NX):
                start = (z * NX + x) * 16
                out_ref[x, z // 4, z % 4] = total[start : start + 16]


def first(coef, high, low, passed):
    occ, depth = coef.shape
    width = high.shape[1]
    step = 512
    piece = pl.BlockSpec((step, width), lambda k: (k, 0))
    return pl.pallas_call(
        first_kernel,
        out_shape=(
            jax.ShapeDtypeStruct((NX, 2, 4, 16, width), F32),
            jax.ShapeDtypeStruct(passed.shape, passed.dtype),
        ),
        grid=(depth // step,),
        in_specs=[
            pl.BlockSpec((occ, step), lambda k: (0, k)),
            piece,
            piece,
            pl.BlockSpec(memory_space=pl.ANY),
        ],
        out_specs=(
            pl.BlockSpec((NX, 2, 4, 16, width), lambda k: (0, 0, 0, 0, 0)),
            pl.BlockSpec(memory_space=pl.ANY),
        ),
        input_output_aliases={3: 1},
        scratch_shapes=[pltpu.VMEM((occ, width), F32)],
        compiler_params=pltpu.CompilerParams(vmem_limit_bytes=56 * 2**20),
        cost_estimate=pl.CostEstimate(
            flops=6 * occ * depth * width, bytes_accessed=14 * 2**20, transcendentals=0
        ),
    )(coef, high, low, passed)


def second_kernel(core_ref, own_ref, other_ref, half_ref, out_ref):
    core = core_ref[0]
    half = half_ref[...]
    width = half.shape[1] // 2
    half = jnp.concatenate([half[:, :width], half[:, width:]], axis=0)
    half_high, half_low = split(half)

    def dot(a, b):
        return lax.dot_general(a, b, (((1,), (1,)), ((), ())), preferred_element_type=F32)

    for which, ref in ((core, own_ref), (1 - core, other_ref)):
        high, low = split(ref[...])
        part = (dot(high, half_low) + dot(low, half_high)) + dot(high, half_high)
        out_ref[:, pl.ds(which, 1)] = part.reshape(NX * NZ, 1, 16, part.shape[1])


def second(core, own, other, half):
    vmem = pl.BlockSpec(memory_space=pltpu.VMEM)
    return pl.pallas_call(
        second_kernel,
        out_shape=jax.ShapeDtypeStruct((NX * NZ, 2, 16, 2 * half.shape[0]), F32),
        in_specs=[pl.BlockSpec(memory_space=pltpu.SMEM), vmem, vmem, vmem],
        compiler_params=pltpu.CompilerParams(vmem_limit_bytes=32 * 2**20),
    )(core, own, other, half)


def last_kernel(parts_ref, out_ref):
    count = parts_ref.shape[0] // 2
    sums = [parts_ref[core] for core in range(2)]
    for place in range(1, count):
        for core in range(2):
            sums[core] += parts_ref[2 * place + core]
    for aux in range(2):
        runs = [sums[core][:, aux * 64 + z * 16 :][:, :16] for z in range(4) for core in range(2)]
        out_ref[aux] = jnp.concatenate(runs, axis=1)


def last(parts):
    return pl.pallas_call(
        last_kernel,
        out_shape=jax.ShapeDtypeStruct((2, parts.shape[1], parts.shape[2]), F32),
    )(parts)


def shards(integrals, coefs, screen, domains):
    aux, row_len, col_len = integrals.shape
    occ = coefs.shape[1]
    row, core = lax.axis_index("y"), lax.axis_index("core")
    col = lax.axis_index(("x", "z", "core"))
    row_tiles = row_len // TILE

    tile_ids = row * row_tiles + jnp.arange(row_tiles, dtype=jnp.int32)
    listed = lax.dynamic_index_in_dim(domains, col * occ // TILE, 0, keepdims=False)
    in_domain = jnp.any(listed[None, :] == tile_ids[:, None], axis=1).astype(F32)
    coef = coefs.T * jnp.repeat(in_domain, TILE)[None, :]

    along_x = gather(coef, "x")
    gathered = lax.all_gather(along_x.reshape(NX * occ, row_len), "z", axis=0, tiled=True)

    keep = screen.astype(F32)
    screened = (
        integrals.reshape(aux, row_tiles, TILE, col_len // TILE, TILE) * keep[None, :, None, :, None]
    ).reshape(integrals.shape)
    high, low = pieces(core[None], screened, swap(screened))

    chip_len = 2 * col_len
    mine = lax.dynamic_index_in_dim(along_x, lax.axis_index("x"), 0, keepdims=False)
    along_y = gather(mine, "y").reshape(8, occ, row_len // chip_len, chip_len)
    along_y = along_y.transpose(0, 2, 1, 3).reshape(NX * NZ, occ, chip_len)

    half, along_y = first(gathered, high, low, along_y)
    half = half.reshape(NX * NZ * occ, 2 * aux * col_len)
    half = lax.psum_scatter(half, "y", scatter_dimension=0, tiled=True)

    rows = lax.all_to_all(along_y, ("x", "z"), 0, 0, tiled=True).reshape(NX * NZ * occ, chip_len)
    pairs = second(core[None], rows, swap(rows), half)
    pairs = pairs.reshape(NX * NZ * 2, occ, pairs.shape[3])
    pairs = lax.all_to_all(pairs, ("x", "z", "core"), 0, 0, tiled=True)
    return last(pairs).transpose(0, 2, 1)


def solution(mesh):
    devices = mesh.devices.reshape(8, NX, NZ, 2)
    split_mesh = Mesh(devices, ("y", "x", "z", "core"))
    col = ("x", "z", "core")
    placed = (P(None, "y", col), P("y", col), P("y", col), P())
    return jax.shard_map(
        shards, mesh=split_mesh, in_specs=placed, out_specs=P(None, "y", col), check_vma=False
    )
```

```python
import jax
import jax.numpy as jnp
from jax import lax
from jax.experimental import pallas as pl
from jax.experimental.pallas import tpu as pltpu
from jax.sharding import Mesh, PartitionSpec as P

TILE = 128
NX, NZ = 4, 8
BF16 = jnp.bfloat16
F32 = jnp.float32


def split(value):
    high = value.astype(BF16)
    return high, (value - high.astype(F32)).astype(BF16)


def swap(value):
    return lax.ppermute(value, "core", [(0, 1), (1, 0)])


def gather(value, axis):
    copies = jnp.broadcast_to(value[None], (lax.axis_size(axis),) + value.shape)
    return lax.all_to_all(copies, axis, 0, 0, tiled=True)


def first_kernel(coef_ref, own_ref, other_ref, passed_ref, out_ref, passed_out_ref, total):
    del passed_ref, passed_out_ref
    step = pl.program_id(0)
    aux, _, width = own_ref.shape
    coef_high, coef_low = split(coef_ref[...])

    @pl.when(step == 0)
    def _():
        total[...] = jnp.zeros_like(total)

    for p in range(aux):
        for place, ref in enumerate((own_ref, other_ref)):
            high, low = split(ref[p])
            part = jnp.dot(coef_high, low, preferred_element_type=F32)
            part += jnp.dot(coef_low, high, preferred_element_type=F32)
            part += jnp.dot(coef_high, high, preferred_element_type=F32)
            start = (2 * p + place) * width
            total[:, start : start + width] += part

    @pl.when(step == pl.num_programs(0) - 1)
    def _():
        for z in range(NZ):
            for x in range(NX):
                start = (z * NX + x) * 16
                out_ref[x, z // 4, z % 4] = total[start : start + 16]


def first(coef, own, other, passed):
    occ, depth = coef.shape
    aux, _, half_width = own.shape
    width = 2 * aux * half_width
    step = 512
    block = pl.BlockSpec((aux, step, half_width), lambda k: (0, k, 0))
    return pl.pallas_call(
        first_kernel,
        out_shape=(
            jax.ShapeDtypeStruct((NX, 2, 4, 16, width), F32),
            jax.ShapeDtypeStruct(passed.shape, passed.dtype),
        ),
        grid=(depth // step,),
        in_specs=[
            pl.BlockSpec((occ, step), lambda k: (0, k)),
            block,
            block,
            pl.BlockSpec(memory_space=pl.ANY),
        ],
        out_specs=(
            pl.BlockSpec((NX, 2, 4, 16, width), lambda k: (0, 0, 0, 0, 0)),
            pl.BlockSpec(memory_space=pl.ANY),
        ),
        input_output_aliases={3: 1},
        scratch_shapes=[pltpu.VMEM((occ, width), F32)],
        compiler_params=pltpu.CompilerParams(vmem_limit_bytes=56 * 2**20),
        cost_estimate=pl.CostEstimate(
            flops=6 * occ * depth * width, bytes_accessed=14 * 2**20, transcendentals=0
        ),
    )(coef, own, other, passed)


def second_kernel(core_ref, own_ref, other_ref, half_ref, out_ref):
    core = core_ref[0]
    half = half_ref[...]
    width = half.shape[1] // 4
    own, other = (
        jnp.concatenate([half[:, n * width : (n + 1) * width] for n in (place, place + 2)], axis=0)
        for place in range(2)
    )
    half = jnp.concatenate([jnp.where(core == 0, own, other), jnp.where(core == 0, other, own)], axis=1)
    half_high, half_low = split(half)

    def dot(a, b):
        return lax.dot_general(a, b, (((1,), (1,)), ((), ())), preferred_element_type=F32)

    for which, ref in ((core, own_ref), (1 - core, other_ref)):
        high, low = split(ref[...])
        part = (dot(high, half_low) + dot(low, half_high)) + dot(high, half_high)
        out_ref[:, pl.ds(which, 1)] = part.reshape(NX * NZ, 1, 16, part.shape[1])


def second(core, own, other, half):
    vmem = pl.BlockSpec(memory_space=pltpu.VMEM)
    return pl.pallas_call(
        second_kernel,
        out_shape=jax.ShapeDtypeStruct((NX * NZ, 2, 16, 2 * half.shape[0]), F32),
        in_specs=[pl.BlockSpec(memory_space=pltpu.SMEM), vmem, vmem, vmem],
        compiler_params=pltpu.CompilerParams(vmem_limit_bytes=32 * 2**20),
    )(core, own, other, half)


def last_kernel(parts_ref, out_ref):
    count = parts_ref.shape[0] // 2
    sums = [parts_ref[core] for core in range(2)]
    for place in range(1, count):
        for core in range(2):
            sums[core] += parts_ref[2 * place + core]
    for aux in range(2):
        runs = [sums[core][:, aux * 64 + z * 16 :][:, :16] for z in range(4) for core in range(2)]
        out_ref[aux] = jnp.concatenate(runs, axis=1)


def last(parts):
    return pl.pallas_call(
        last_kernel,
        out_shape=jax.ShapeDtypeStruct((2, parts.shape[1], parts.shape[2]), F32),
    )(parts)


def shards(integrals, coefs, screen, domains):
    aux, row_len, col_len = integrals.shape
    occ = coefs.shape[1]
    row, core = lax.axis_index("y"), lax.axis_index("core")
    col = lax.axis_index(("x", "z", "core"))
    row_tiles = row_len // TILE

    tile_ids = row * row_tiles + jnp.arange(row_tiles, dtype=jnp.int32)
    listed = lax.dynamic_index_in_dim(domains, col * occ // TILE, 0, keepdims=False)
    in_domain = jnp.any(listed[None, :] == tile_ids[:, None], axis=1).astype(F32)
    coef = coefs.T * jnp.repeat(in_domain, TILE)[None, :]

    along_x = gather(coef, "x")
    gathered = lax.all_gather(along_x.reshape(NX * occ, row_len), "z", axis=0, tiled=True)

    keep = screen.astype(F32)
    screened = (
        integrals.reshape(aux, row_tiles, TILE, col_len // TILE, TILE) * keep[None, :, None, :, None]
    ).reshape(integrals.shape)
    other = swap(screened)

    chip_len = 2 * col_len
    mine = lax.dynamic_index_in_dim(along_x, lax.axis_index("x"), 0, keepdims=False)
    along_y = gather(mine, "y").reshape(8, occ, row_len // chip_len, chip_len)
    along_y = along_y.transpose(0, 2, 1, 3).reshape(NX * NZ, occ, chip_len)

    half, along_y = first(gathered, screened, other, along_y)
    half = half.reshape(NX * NZ * occ, 2 * aux * col_len)
    half = lax.psum_scatter(half, "y", scatter_dimension=0, tiled=True)

    rows = lax.all_to_all(along_y, ("x", "z"), 0, 0, tiled=True).reshape(NX * NZ * occ, chip_len)
    pairs = second(core[None], rows, swap(rows), half)
    pairs = pairs.reshape(NX, NZ * 2, occ, pairs.shape[3])
    pairs = lax.all_to_all(pairs, "x", 0, 0, tiled=True).sum(axis=0)
    pairs = lax.all_to_all(pairs, ("z", "core"), 0, 0, tiled=True)
    return last(pairs).transpose(0, 2, 1)


def solution(mesh):
    devices = mesh.devices.reshape(8, NX, NZ, 2)
    split_mesh = Mesh(devices, ("y", "x", "z", "core"))
    col = ("x", "z", "core")
    placed = (P(None, "y", col), P("y", col), P("y", col), P())
    return jax.shard_map(
        shards, mesh=split_mesh, in_specs=placed, out_specs=P(None, "y", col), check_vma=False
    )
```

```python
import jax
import jax.numpy as jnp
from jax import lax
from jax.experimental import pallas as pl
from jax.experimental.pallas import tpu as pltpu
from jax.sharding import Mesh, PartitionSpec as P

TILE = 128
NX, NZ = 4, 8
BF16 = jnp.bfloat16
F32 = jnp.float32


def split(value):
    high = value.astype(BF16)
    return high, (value - high.astype(F32)).astype(BF16)


def swap(value):
    return lax.ppermute(value, "core", [(0, 1), (1, 0)])


def gather(value, axis):
    copies = jnp.broadcast_to(value[None], (lax.axis_size(axis),) + value.shape)
    return lax.all_to_all(copies, axis, 0, 0, tiled=True)


def first_kernel(coef_ref, own_ref, other_ref, passed_ref, out_ref, passed_out_ref, total):
    del passed_ref, passed_out_ref
    step = pl.program_id(0)
    aux, _, width = own_ref.shape
    coef_high, coef_low = split(coef_ref[...])

    @pl.when(step == 0)
    def _():
        total[...] = jnp.zeros_like(total)

    for p in range(aux):
        for place, ref in enumerate((own_ref, other_ref)):
            high, low = split(ref[p])
            part = jnp.dot(coef_high, low, preferred_element_type=F32)
            part += jnp.dot(coef_low, high, preferred_element_type=F32)
            part += jnp.dot(coef_high, high, preferred_element_type=F32)
            start = (2 * p + place) * width
            total[:, start : start + width] += part

    @pl.when(step == pl.num_programs(0) - 1)
    def _():
        for z in range(NZ):
            for x in range(NX):
                start = (z * NX + x) * 16
                out_ref[x, z // 4, z % 4] = total[start : start + 16]


def first(coef, own, other, passed):
    occ, depth = coef.shape
    aux, _, half_width = own.shape
    width = 2 * aux * half_width
    step = 512
    block = pl.BlockSpec((aux, step, half_width), lambda k: (0, k, 0))
    return pl.pallas_call(
        first_kernel,
        out_shape=(
            jax.ShapeDtypeStruct((NX, 2, 4, 16, width), F32),
            jax.ShapeDtypeStruct(passed.shape, passed.dtype),
        ),
        grid=(depth // step,),
        in_specs=[
            pl.BlockSpec((occ, step), lambda k: (0, k)),
            block,
            block,
            pl.BlockSpec(memory_space=pl.ANY),
        ],
        out_specs=(
            pl.BlockSpec((NX, 2, 4, 16, width), lambda k: (0, 0, 0, 0, 0)),
            pl.BlockSpec(memory_space=pl.ANY),
        ),
        input_output_aliases={3: 1},
        scratch_shapes=[pltpu.VMEM((occ, width), F32)],
        compiler_params=pltpu.CompilerParams(vmem_limit_bytes=56 * 2**20),
        cost_estimate=pl.CostEstimate(
            flops=6 * occ * depth * width, bytes_accessed=14 * 2**20, transcendentals=0
        ),
    )(coef, own, other, passed)


def second_kernel(rows_ref, halves_ref, out_ref):
    width = halves_ref.shape[2] // 4

    def nus(p, z, source):
        pair = halves_ref[source, z * 16 : z * 16 + 16, 2 * p * width : 2 * (p + 1) * width]
        return pair if source == 0 else jnp.concatenate([pair[:, width:], pair[:, :width]], axis=1)

    half = jnp.concatenate([nus(p, z, c) for p in range(2) for z in range(4) for c in range(2)], axis=0)
    half_high, half_low = split(half)
    rows_high, rows_low = split(rows_ref[...])

    def dot(a, b):
        return lax.dot_general(a, b, (((1,), (1,)), ((), ())), preferred_element_type=F32)

    out_ref[...] = (dot(rows_high, half_low) + dot(rows_low, half_high)) + dot(rows_high, half_high)


def second(rows, halves):
    vmem = pl.BlockSpec(memory_space=pltpu.VMEM)
    return pl.pallas_call(
        second_kernel,
        out_shape=jax.ShapeDtypeStruct((rows.shape[0], 4 * halves.shape[1]), F32),
        in_specs=[vmem, vmem],
        compiler_params=pltpu.CompilerParams(vmem_limit_bytes=32 * 2**20),
    )(rows, halves)


def last_kernel(parts_ref, out_ref):
    total = parts_ref[0]
    for place in range(1, parts_ref.shape[0]):
        total += parts_ref[place]
    width = out_ref.shape[2]
    for aux in range(2):
        out_ref[aux] = total[:, aux * width : (aux + 1) * width]


def last(parts):
    return pl.pallas_call(
        last_kernel,
        out_shape=jax.ShapeDtypeStruct((2, parts.shape[1], parts.shape[2] // 2), F32),
    )(parts)


def shards(integrals, coefs, screen, domains):
    aux, row_len, col_len = integrals.shape
    occ = coefs.shape[1]
    row = lax.axis_index("y")
    col = lax.axis_index(("x", "z", "core"))
    row_tiles = row_len // TILE

    tile_ids = row * row_tiles + jnp.arange(row_tiles, dtype=jnp.int32)
    listed = lax.dynamic_index_in_dim(domains, col * occ // TILE, 0, keepdims=False)
    in_domain = jnp.any(listed[None, :] == tile_ids[:, None], axis=1).astype(F32)
    coef = coefs.T * jnp.repeat(in_domain, TILE)[None, :]

    along_x = gather(coef, "x")
    gathered = lax.all_gather(along_x.reshape(NX * occ, row_len), "z", axis=0, tiled=True)

    keep = screen.astype(F32)
    screened = (
        integrals.reshape(aux, row_tiles, TILE, col_len // TILE, TILE) * keep[None, :, None, :, None]
    ).reshape(integrals.shape)
    other = swap(screened)

    chip_len = 2 * col_len
    mine = lax.dynamic_index_in_dim(along_x, lax.axis_index("x"), 0, keepdims=False)
    along_y = gather(mine, "y").reshape(8, occ, row_len // chip_len, chip_len)
    along_y = along_y.transpose(0, 2, 1, 3).reshape(NX * NZ, occ, chip_len)

    half, along_y = first(gathered, screened, other, along_y)
    half = half.reshape(NX * NZ * occ, 2 * aux * col_len)
    half = lax.psum_scatter(half, "y", scatter_dimension=0, tiled=True)

    rows = lax.all_to_all(along_y, ("x", "z"), 0, 0, tiled=True).reshape(NX * NZ * occ, chip_len)
    pairs = second(rows, lax.all_gather(half, "core"))
    pairs = pairs.reshape(NX * NZ, occ, pairs.shape[1])
    pairs = lax.all_to_all(pairs, ("x", "z"), 0, 0, tiled=True)
    return last(pairs).transpose(0, 2, 1)


def solution(mesh):
    devices = mesh.devices.reshape(8, NX, NZ, 2)
    split_mesh = Mesh(devices, ("y", "x", "z", "core"))
    col = ("x", "z", "core")
    placed = (P(None, "y", col), P("y", col), P("y", col), P())
    return jax.shard_map(
        shards, mesh=split_mesh, in_specs=placed, out_specs=P(None, "y", col), check_vma=False
    )
```

```python
import jax
import jax.numpy as jnp
from jax import lax
from jax.experimental import pallas as pl
from jax.experimental.pallas import tpu as pltpu
from jax.sharding import Mesh, PartitionSpec as P

TILE = 128
NX, NZ = 4, 8
REST = 256
BF16 = jnp.bfloat16
F32 = jnp.float32


def split(value):
    high = value.astype(BF16)
    return high, (value - high.astype(F32)).astype(BF16)


def swap(value):
    return lax.ppermute(value, "core", [(0, 1), (1, 0)])


def gather(value, axis):
    copies = jnp.broadcast_to(value[None], (lax.axis_size(axis),) + value.shape)
    return lax.all_to_all(copies, axis, 0, 0, tiled=True)


def around(value, axis):
    count = lax.axis_size(axis)
    found = [value] * count
    for step in range(1, count // 2 + 1):
        found[step] = lax.ppermute(found[step - 1], axis, [(i, (i - 1) % count) for i in range(count)])
        if 2 * step < count:
            back = found[(1 - step) % count]
            found[-step] = lax.ppermute(back, axis, [(i, (i + 1) % count) for i in range(count)])
    return jnp.stack(found)


def first_kernel(
    coef_hbm, rest_hbm, own_hbm, other_hbm, passed_hbm, out_hbm, passed_out_hbm,
    coef, rest, own, other, total, sums, coef_sem, rest_sem, own_sem, other_sem, out_sem,
):
    del passed_hbm, passed_out_hbm
    steps, aux, depth, width = own.shape

    def copies(step):
        rows = pl.ds(step * depth, depth)
        if step < steps - 1:
            columns = pltpu.make_async_copy(coef_hbm.at[:, rows], coef.at[step], coef_sem.at[step])
        else:
            columns = pltpu.make_async_copy(rest_hbm, rest, rest_sem)
        return (
            columns,
            pltpu.make_async_copy(own_hbm.at[:, rows, :], own.at[step], own_sem.at[step]),
            pltpu.make_async_copy(other_hbm.at[:, rows, :], other.at[step], other_sem.at[step]),
        )

    for step in range(steps):
        for copy in copies(step):
            copy.start()
    for step in range(steps):
        for copy in copies(step):
            copy.wait()
        coef_high, coef_low = split(coef[step] if step < steps - 1 else rest[...])
        for p in range(aux):
            for place, integrals in enumerate((own, other)):
                high, low = split(integrals[step, p])
                part = jnp.dot(coef_high, low, preferred_element_type=F32)
                part += jnp.dot(coef_low, high, preferred_element_type=F32)
                part += jnp.dot(coef_high, high, preferred_element_type=F32)
                columns = slice((2 * p + place) * width, (2 * p + place + 1) * width)
                if step == 0:
                    total[:, columns] = part
                elif step < steps - 1:
                    total[:, columns] += part
                else:
                    for z in range(NZ):
                        for x in range(NX):
                            start, end = (z * NX + x) * 16, (x * NZ + z) * 16
                            sums[end : end + 16, columns] = total[start : start + 16, columns] + part[end : end + 16]
    copy = pltpu.make_async_copy(sums, out_hbm, out_sem)
    copy.start()
    copy.wait()


def first(coef, rest, own, other, passed):
    occ = coef.shape[0]
    aux, full_depth, half_width = own.shape
    depth = rest.shape[1]
    steps = full_depth // depth
    width = 2 * aux * half_width
    away = pl.BlockSpec(memory_space=pl.ANY)
    block = pltpu.VMEM((steps, aux, depth, half_width), F32)
    sems = pltpu.SemaphoreType.DMA((steps,))
    return pl.pallas_call(
        first_kernel,
        out_shape=(
            jax.ShapeDtypeStruct((occ, width), F32),
            jax.ShapeDtypeStruct(passed.shape, passed.dtype),
        ),
        in_specs=[away] * 5,
        out_specs=(away, away),
        input_output_aliases={4: 1},
        scratch_shapes=[
            pltpu.VMEM((steps - 1, occ, depth), F32),
            pltpu.VMEM((occ, depth), F32),
            block,
            block,
            pltpu.VMEM((occ, width), F32),
            pltpu.VMEM((occ, width), F32),
            pltpu.SemaphoreType.DMA((steps - 1,)),
            pltpu.SemaphoreType.DMA,
            sems,
            sems,
            pltpu.SemaphoreType.DMA,
        ],
        compiler_params=pltpu.CompilerParams(vmem_limit_bytes=56 * 2**20),
        cost_estimate=pl.CostEstimate(
            flops=6 * occ * full_depth * width, bytes_accessed=14 * 2**20, transcendentals=0
        ),
    )(coef, rest, own, other, passed)


def second_kernel(rows_ref, halves_ref, out_ref):
    width = halves_ref.shape[2] // 4

    def nus(p, z, source):
        pair = halves_ref[source, z * 16 : z * 16 + 16, 2 * p * width : 2 * (p + 1) * width]
        return pair if source == 0 else jnp.concatenate([pair[:, width:], pair[:, :width]], axis=1)

    half = jnp.concatenate([nus(p, z, c) for p in range(2) for z in range(4) for c in range(2)], axis=0)
    half_high, half_low = split(half)
    rows_high, rows_low = split(rows_ref[...])

    def dot(a, b):
        return lax.dot_general(a, b, (((1,), (1,)), ((), ())), preferred_element_type=F32)

    out_ref[...] = (dot(rows_high, half_low) + dot(rows_low, half_high)) + dot(rows_high, half_high)


def second(rows, halves):
    vmem = pl.BlockSpec(memory_space=pltpu.VMEM)
    return pl.pallas_call(
        second_kernel,
        out_shape=jax.ShapeDtypeStruct((rows.shape[0], 4 * halves.shape[1]), F32),
        in_specs=[vmem, vmem],
        compiler_params=pltpu.CompilerParams(vmem_limit_bytes=32 * 2**20),
    )(rows, halves)


def last_kernel(parts_ref, out_ref):
    total = parts_ref[0]
    for place in range(1, parts_ref.shape[0]):
        total += parts_ref[place]
    width = out_ref.shape[2]
    for aux in range(2):
        out_ref[aux] = total[:, aux * width : (aux + 1) * width]


def last(parts):
    return pl.pallas_call(
        last_kernel,
        out_shape=jax.ShapeDtypeStruct((2, parts.shape[1], parts.shape[2] // 2), F32),
    )(parts)


def shards(integrals, coefs, screen, domains):
    aux, row_len, col_len = integrals.shape
    occ = coefs.shape[1]
    row = lax.axis_index("y")
    col = lax.axis_index(("x", "z", "core"))
    row_tiles = row_len // TILE

    tile_ids = row * row_tiles + jnp.arange(row_tiles, dtype=jnp.int32)
    listed = lax.dynamic_index_in_dim(domains, col * occ // TILE, 0, keepdims=False)
    in_domain = jnp.any(listed[None, :] == tile_ids[:, None], axis=1).astype(F32)
    coef = coefs.T * jnp.repeat(in_domain, TILE)[None, :]

    most = row_len - REST
    along_x = gather(coef[:, :most], "x")
    gathered = lax.all_gather(along_x.reshape(NX * occ, most), "z", axis=0, tiled=True)

    keep = screen.astype(F32)
    screened = (
        integrals.reshape(aux, row_tiles, TILE, col_len // TILE, TILE) * keep[None, :, None, :, None]
    ).reshape(integrals.shape)
    other = swap(screened)

    after = 0.0 * (along_x[0, 0, 0] + screened[0, 0, 0])
    rest = gather(gather(coef[:, most:] + after, "z"), "x").reshape(NX * NZ * occ, REST)

    along_y = around(coef + 0.0 * along_x[0, 0, 0], "y")

    half, along_y = first(gathered, rest, screened, other, along_y)
    half = lax.psum_scatter(half, "y", scatter_dimension=0, tiled=True)

    chip_len = 2 * col_len
    along_y = lax.dynamic_slice_in_dim(jnp.concatenate([along_y, along_y]), lax.rem(8 - row, 8), 8, 0)
    along_y = along_y.reshape(8, occ, row_len // chip_len, chip_len).transpose(0, 2, 1, 3)
    rows = lax.all_to_all(along_y.reshape(NX * NZ, occ, chip_len), ("x", "z"), 0, 0, tiled=True)
    pairs = second(rows.reshape(NX * NZ * occ, chip_len), lax.all_gather(half, "core"))
    pairs = pairs.reshape(NX * NZ, occ, pairs.shape[1])
    pairs = lax.all_to_all(pairs, ("x", "z"), 0, 0, tiled=True)
    return last(pairs).transpose(0, 2, 1)


def solution(mesh):
    devices = mesh.devices.reshape(8, NX, NZ, 2)
    split_mesh = Mesh(devices, ("y", "x", "z", "core"))
    col = ("x", "z", "core")
    placed = (P(None, "y", col), P("y", col), P("y", col), P())
    return jax.shard_map(
        shards, mesh=split_mesh, in_specs=placed, out_specs=P(None, "y", col), check_vma=False
    )
```

```python
import jax
import jax.numpy as jnp
from jax import lax
from jax.experimental import pallas as pl
from jax.experimental.pallas import tpu as pltpu
from jax.sharding import Mesh, PartitionSpec as P

TILE = 128
NX, NZ = 4, 8
REST, CHUNK = 256, 256
BF16 = jnp.bfloat16
F32 = jnp.float32


def split(value):
    high = value.astype(BF16)
    return high, (value - high.astype(F32)).astype(BF16)


def swap(value):
    return lax.ppermute(value, "core", [(0, 1), (1, 0)])


def gather(value, axis):
    copies = jnp.broadcast_to(value[None], (lax.axis_size(axis),) + value.shape)
    return lax.all_to_all(copies, axis, 0, 0, tiled=True)


def around(value, axis):
    count = lax.axis_size(axis)
    found = [value] * count
    for step in range(1, count // 2 + 1):
        found[step] = lax.ppermute(found[step - 1], axis, [(i, (i - 1) % count) for i in range(count)])
        if 2 * step < count:
            back = found[(1 - step) % count]
            found[-step] = lax.ppermute(back, axis, [(i, (i + 1) % count) for i in range(count)])
    return jnp.stack(found)


def first_kernel(
    own_screen, other_screen, coef_hbm, rest_hbm, own_hbm, other_hbm, passed_hbm, out_hbm, passed_out_hbm,
    coef, rest, own, other, total, sums, coef_sem, own_sem, other_sem, out_sem,
):
    del passed_hbm, passed_out_hbm
    aux, full_depth, width = own.shape
    most = coef.shape[1]
    starts = [*range(0, most, CHUNK), most]
    ends = [*starts[1:], full_depth]

    def copies(step):
        rows = pl.ds(starts[step], ends[step] - starts[step])
        if starts[step] < most:
            columns = pltpu.make_async_copy(coef_hbm.at[:, rows], coef.at[:, rows], coef_sem.at[step])
        else:
            columns = pltpu.make_async_copy(rest_hbm, rest, coef_sem.at[step])
        return (
            columns,
            pltpu.make_async_copy(own_hbm.at[:, rows, :], own.at[:, rows, :], own_sem.at[step]),
            pltpu.make_async_copy(other_hbm.at[:, rows, :], other.at[:, rows, :], other_sem.at[step]),
        )

    def screened(integrals, screen, p, start, end):
        def tile(row, column):
            block = integrals[p, row * TILE : (row + 1) * TILE, column * TILE : (column + 1) * TILE]
            return block * screen[row, column].astype(F32)

        return jnp.concatenate(
            [
                jnp.concatenate([tile(row, column) for column in range(width // TILE)], axis=1)
                for row in range(start // TILE, end // TILE)
            ],
            axis=0,
        )

    for step in range(len(starts)):
        for copy in copies(step):
            copy.start()
    for step, (first_row, end_row) in enumerate(zip(starts, ends, strict=True)):
        for copy in copies(step):
            copy.wait()
        coef_high, coef_low = split(coef[:, first_row:end_row] if first_row < most else rest[...])
        for p in range(aux):
            for place, (integrals, screen) in enumerate(((own, own_screen), (other, other_screen))):
                high, low = split(screened(integrals, screen, p, first_row, end_row))
                part = jnp.dot(coef_high, low, preferred_element_type=F32)
                part += jnp.dot(coef_low, high, preferred_element_type=F32)
                part += jnp.dot(coef_high, high, preferred_element_type=F32)
                columns = slice((2 * p + place) * width, (2 * p + place + 1) * width)
                if step == 0:
                    total[:, columns] = part
                elif first_row < most:
                    total[:, columns] += part
                else:
                    for z in range(NZ):
                        for x in range(NX):
                            start, end = (z * NX + x) * 16, (x * NZ + z) * 16
                            sums[end : end + 16, columns] = total[start : start + 16, columns] + part[end : end + 16]
    copy = pltpu.make_async_copy(sums, out_hbm, out_sem)
    copy.start()
    copy.wait()


def first(own_screen, other_screen, coef, rest, own, other, passed):
    occ, most = coef.shape
    aux, full_depth, half_width = own.shape
    steps = most // CHUNK + 1
    width = 2 * aux * half_width
    away, scalars = pl.BlockSpec(memory_space=pl.ANY), pl.BlockSpec(memory_space=pltpu.SMEM)
    sems = pltpu.SemaphoreType.DMA((steps,))
    return pl.pallas_call(
        first_kernel,
        out_shape=(
            jax.ShapeDtypeStruct((occ, width), F32),
            jax.ShapeDtypeStruct(passed.shape, passed.dtype),
        ),
        in_specs=[scalars, scalars] + [away] * 5,
        out_specs=(away, away),
        input_output_aliases={6: 1},
        scratch_shapes=[
            pltpu.VMEM(coef.shape, F32),
            pltpu.VMEM(rest.shape, F32),
            pltpu.VMEM(own.shape, F32),
            pltpu.VMEM(other.shape, F32),
            pltpu.VMEM((occ, width), F32),
            pltpu.VMEM((occ, width), F32),
            sems,
            sems,
            sems,
            pltpu.SemaphoreType.DMA,
        ],
        compiler_params=pltpu.CompilerParams(vmem_limit_bytes=56 * 2**20),
        cost_estimate=pl.CostEstimate(
            flops=6 * occ * full_depth * width, bytes_accessed=14 * 2**20, transcendentals=0
        ),
    )(own_screen, other_screen, coef, rest, own, other, passed)


def second_kernel(rows_ref, halves_ref, out_ref):
    width = halves_ref.shape[2] // 4

    def nus(p, z, source):
        pair = halves_ref[source, z * 16 : z * 16 + 16, 2 * p * width : 2 * (p + 1) * width]
        return pair if source == 0 else jnp.concatenate([pair[:, width:], pair[:, :width]], axis=1)

    half = jnp.concatenate([nus(p, z, c) for p in range(2) for z in range(4) for c in range(2)], axis=0)
    half_high, half_low = split(half)
    rows_high, rows_low = split(rows_ref[...])

    def dot(a, b):
        return lax.dot_general(a, b, (((1,), (1,)), ((), ())), preferred_element_type=F32)

    out_ref[...] = (dot(rows_high, half_low) + dot(rows_low, half_high)) + dot(rows_high, half_high)


def second(rows, halves):
    vmem = pl.BlockSpec(memory_space=pltpu.VMEM)
    return pl.pallas_call(
        second_kernel,
        out_shape=jax.ShapeDtypeStruct((rows.shape[0], 4 * halves.shape[1]), F32),
        in_specs=[vmem, vmem],
        compiler_params=pltpu.CompilerParams(vmem_limit_bytes=32 * 2**20),
    )(rows, halves)


def last_kernel(parts_ref, out_ref):
    total = parts_ref[0]
    for place in range(1, parts_ref.shape[0]):
        total += parts_ref[place]
    width = out_ref.shape[2]
    for aux in range(2):
        out_ref[aux] = total[:, aux * width : (aux + 1) * width]


def last(parts):
    return pl.pallas_call(
        last_kernel,
        out_shape=jax.ShapeDtypeStruct((2, parts.shape[1], parts.shape[2] // 2), F32),
    )(parts)


def shards(integrals, coefs, screen, domains):
    aux, row_len, col_len = integrals.shape
    occ = coefs.shape[1]
    row = lax.axis_index("y")
    col = lax.axis_index(("x", "z", "core"))
    row_tiles = row_len // TILE

    tile_ids = row * row_tiles + jnp.arange(row_tiles, dtype=jnp.int32)
    listed = lax.dynamic_index_in_dim(domains, col * occ // TILE, 0, keepdims=False)
    in_domain = jnp.any(listed[None, :] == tile_ids[:, None], axis=1).astype(F32)
    coef = coefs.T * jnp.repeat(in_domain, TILE)[None, :]

    most = row_len - REST
    along_x = gather(coef[:, :most], "x")
    gathered = lax.all_gather(along_x.reshape(NX * occ, most), "z", axis=0, tiled=True)

    rest = gather(gather(coef[:, most:] + 0.0 * along_x[0, :, :REST], "z"), "x").reshape(NX * NZ * occ, REST)

    along_y = around(coef + 0.0 * jnp.pad(along_x[0], ((0, 0), (0, REST))), "y")

    half, along_y = first(screen, swap(screen), gathered, rest, integrals, swap(integrals), along_y)
    half = lax.psum_scatter(half, "y", scatter_dimension=0, tiled=True)

    chip_len = 2 * col_len
    along_y = lax.dynamic_slice_in_dim(jnp.concatenate([along_y, along_y]), lax.rem(8 - row, 8), 8, 0)
    along_y = along_y.reshape(8, occ, row_len // chip_len, chip_len).transpose(0, 2, 1, 3)
    rows = lax.all_to_all(along_y.reshape(NX * NZ, occ, chip_len), ("x", "z"), 0, 0, tiled=True)
    pairs = second(rows.reshape(NX * NZ * occ, chip_len), lax.all_gather(half, "core"))
    pairs = pairs.reshape(NX * NZ, occ, pairs.shape[1])
    pairs = lax.all_to_all(pairs, ("x", "z"), 0, 0, tiled=True)
    return last(pairs).transpose(0, 2, 1)


def solution(mesh):
    devices = mesh.devices.reshape(8, NX, NZ, 2)
    split_mesh = Mesh(devices, ("y", "x", "z", "core"))
    col = ("x", "z", "core")
    placed = (P(None, "y", col), P("y", col), P("y", col), P())
    return jax.shard_map(
        shards, mesh=split_mesh, in_specs=placed, out_specs=P(None, "y", col), check_vma=False
    )
```

```python
import jax
import jax.numpy as jnp
from jax import lax
from jax.experimental import pallas as pl
from jax.experimental.pallas import tpu as pltpu
from jax.sharding import Mesh, PartitionSpec as P

TILE = 128
NX, NZ = 4, 8
REST, CHUNK = 512, 256
BF16 = jnp.bfloat16
F32 = jnp.float32


def split(value):
    high = value.astype(BF16)
    return high, (value - high.astype(F32)).astype(BF16)


def swap(value):
    return lax.ppermute(value, "core", [(0, 1), (1, 0)])


def gather(value, axis):
    copies = jnp.broadcast_to(value[None], (lax.axis_size(axis),) + value.shape)
    return lax.all_to_all(copies, axis, 0, 0, tiled=True)


def around(value, axis):
    count = lax.axis_size(axis)
    found = [value] * count
    for step in range(1, count // 2 + 1):
        found[step] = lax.ppermute(found[step - 1], axis, [(i, (i - 1) % count) for i in range(count)])
        if 2 * step < count:
            back = found[(1 - step) % count]
            found[-step] = lax.ppermute(back, axis, [(i, (i + 1) % count) for i in range(count)])
    return jnp.stack(found)


def first_kernel(
    own_screen, other_screen, coef_hbm, rest_hbm, own_hbm, other_hbm, passed_hbm, out_hbm, passed_out_hbm,
    coef, rest, own, other, total, sums, coef_sem, own_sem, other_sem, out_sem,
):
    del passed_hbm, passed_out_hbm
    aux, full_depth, width = own.shape
    most = coef.shape[1]
    starts = [*range(0, most, CHUNK), most]
    ends = [*starts[1:], full_depth]

    def copies(step):
        rows = pl.ds(starts[step], ends[step] - starts[step])
        if starts[step] < most:
            columns = pltpu.make_async_copy(coef_hbm.at[:, rows], coef.at[:, rows], coef_sem.at[step])
        else:
            columns = pltpu.make_async_copy(rest_hbm, rest, coef_sem.at[step])
        return (
            columns,
            pltpu.make_async_copy(own_hbm.at[:, rows, :], own.at[:, rows, :], own_sem.at[step]),
            pltpu.make_async_copy(other_hbm.at[:, rows, :], other.at[:, rows, :], other_sem.at[step]),
        )

    def screened(integrals, screen, p, start, end):
        def tile(row, column):
            block = integrals[p, row * TILE : (row + 1) * TILE, column * TILE : (column + 1) * TILE]
            return block * screen[row, column].astype(F32)

        return jnp.concatenate(
            [
                jnp.concatenate([tile(row, column) for column in range(width // TILE)], axis=1)
                for row in range(start // TILE, end // TILE)
            ],
            axis=0,
        )

    for step in range(len(starts)):
        for copy in copies(step):
            copy.start()
    for step, (first_row, end_row) in enumerate(zip(starts, ends, strict=True)):
        for copy in copies(step):
            copy.wait()
        coef_high, coef_low = split(coef[:, first_row:end_row] if first_row < most else rest[...])
        for p in range(aux):
            for place, (integrals, screen) in enumerate(((own, own_screen), (other, other_screen))):
                high, low = split(screened(integrals, screen, p, first_row, end_row))
                part = jnp.dot(coef_high, low, preferred_element_type=F32)
                part += jnp.dot(coef_low, high, preferred_element_type=F32)
                part += jnp.dot(coef_high, high, preferred_element_type=F32)
                columns = slice((2 * p + place) * width, (2 * p + place + 1) * width)
                if step == 0:
                    total[:, columns] = part
                elif first_row < most:
                    total[:, columns] += part
                else:
                    for z in range(NZ):
                        for x in range(NX):
                            start, end = (z * NX + x) * 16, (x * NZ + z) * 16
                            sums[end : end + 16, columns] = total[start : start + 16, columns] + part[end : end + 16]
    copy = pltpu.make_async_copy(sums, out_hbm, out_sem)
    copy.start()
    copy.wait()


def first(own_screen, other_screen, coef, rest, own, other, passed):
    occ, most = coef.shape
    aux, full_depth, half_width = own.shape
    steps = -(-most // CHUNK) + 1
    width = 2 * aux * half_width
    away, scalars = pl.BlockSpec(memory_space=pl.ANY), pl.BlockSpec(memory_space=pltpu.SMEM)
    sems = pltpu.SemaphoreType.DMA((steps,))
    return pl.pallas_call(
        first_kernel,
        out_shape=(
            jax.ShapeDtypeStruct((occ, width), F32),
            jax.ShapeDtypeStruct(passed.shape, passed.dtype),
        ),
        in_specs=[scalars, scalars] + [away] * 5,
        out_specs=(away, away),
        input_output_aliases={6: 1},
        scratch_shapes=[
            pltpu.VMEM(coef.shape, F32),
            pltpu.VMEM(rest.shape, F32),
            pltpu.VMEM(own.shape, F32),
            pltpu.VMEM(other.shape, F32),
            pltpu.VMEM((occ, width), F32),
            pltpu.VMEM((occ, width), F32),
            sems,
            sems,
            sems,
            pltpu.SemaphoreType.DMA,
        ],
        compiler_params=pltpu.CompilerParams(vmem_limit_bytes=56 * 2**20),
        cost_estimate=pl.CostEstimate(
            flops=6 * occ * full_depth * width, bytes_accessed=14 * 2**20, transcendentals=0
        ),
    )(own_screen, other_screen, coef, rest, own, other, passed)


def second_kernel(rows_ref, halves_ref, out_ref):
    width = halves_ref.shape[2] // 4

    def nus(p, z, source):
        pair = halves_ref[source, z * 16 : z * 16 + 16, 2 * p * width : 2 * (p + 1) * width]
        return pair if source == 0 else jnp.concatenate([pair[:, width:], pair[:, :width]], axis=1)

    half = jnp.concatenate([nus(p, z, c) for p in range(2) for z in range(4) for c in range(2)], axis=0)
    half_high, half_low = split(half)
    rows_high, rows_low = split(rows_ref[...])

    def dot(a, b):
        return lax.dot_general(a, b, (((1,), (1,)), ((), ())), preferred_element_type=F32)

    out_ref[...] = (dot(rows_high, half_low) + dot(rows_low, half_high)) + dot(rows_high, half_high)


def second(rows, halves):
    vmem = pl.BlockSpec(memory_space=pltpu.VMEM)
    return pl.pallas_call(
        second_kernel,
        out_shape=jax.ShapeDtypeStruct((rows.shape[0], 4 * halves.shape[1]), F32),
        in_specs=[vmem, vmem],
        compiler_params=pltpu.CompilerParams(vmem_limit_bytes=32 * 2**20),
    )(rows, halves)


def last_kernel(parts_ref, out_ref):
    total = parts_ref[0]
    for place in range(1, parts_ref.shape[0]):
        total += parts_ref[place]
    width = out_ref.shape[2]
    for aux in range(2):
        out_ref[aux] = total[:, aux * width : (aux + 1) * width]


def last(parts):
    return pl.pallas_call(
        last_kernel,
        out_shape=jax.ShapeDtypeStruct((2, parts.shape[1], parts.shape[2] // 2), F32),
    )(parts)


def shards(integrals, coefs, screen, domains):
    aux, row_len, col_len = integrals.shape
    occ = coefs.shape[1]
    row = lax.axis_index("y")
    col = lax.axis_index(("x", "z", "core"))
    row_tiles = row_len // TILE

    tile_ids = row * row_tiles + jnp.arange(row_tiles, dtype=jnp.int32)
    listed = lax.dynamic_index_in_dim(domains, col * occ // TILE, 0, keepdims=False)
    in_domain = jnp.any(listed[None, :] == tile_ids[:, None], axis=1).astype(F32)
    coef = coefs.T * jnp.repeat(in_domain, TILE)[None, :]

    most = row_len - REST
    along_x = gather(coef[:, :most], "x")
    gathered = lax.all_gather(along_x.reshape(NX * occ, most), "z", axis=0, tiled=True)

    along_z = gather(coef[:, most:] + 0.0 * along_x[0, :, :REST], "z")
    rest = gather(along_z, "x").reshape(NX * NZ * occ, REST)

    along_y = around(coef + 0.0 * jnp.pad(along_z[0], ((0, 0), (0, most))), "y")

    half, along_y = first(screen, swap(screen), gathered, rest, integrals, swap(integrals), along_y)
    half = lax.psum_scatter(half, "y", scatter_dimension=0, tiled=True)

    chip_len = 2 * col_len
    along_y = lax.dynamic_slice_in_dim(jnp.concatenate([along_y, along_y]), lax.rem(8 - row, 8), 8, 0)
    along_y = along_y.reshape(8, occ, row_len // chip_len, chip_len).transpose(0, 2, 1, 3)
    rows = lax.all_to_all(along_y.reshape(NX * NZ, occ, chip_len), ("x", "z"), 0, 0, tiled=True)
    pairs = second(rows.reshape(NX * NZ * occ, chip_len), lax.all_gather(half, "core"))
    pairs = pairs.reshape(NX, NZ, occ, pairs.shape[1])
    pairs = lax.all_to_all(pairs, "x", 0, 0, tiled=True).sum(axis=0)
    pairs = lax.all_to_all(pairs, "z", 0, 0, tiled=True)
    return last(pairs).transpose(0, 2, 1)


def solution(mesh):
    devices = mesh.devices.reshape(8, NX, NZ, 2)
    split_mesh = Mesh(devices, ("y", "x", "z", "core"))
    col = ("x", "z", "core")
    placed = (P(None, "y", col), P("y", col), P("y", col), P())
    return jax.shard_map(
        shards, mesh=split_mesh, in_specs=placed, out_specs=P(None, "y", col), check_vma=False
    )
```

```python
import jax
import jax.numpy as jnp
from jax import lax
from jax.experimental import pallas as pl
from jax.experimental.pallas import tpu as pltpu
from jax.sharding import Mesh, PartitionSpec as P

TILE = 128
NX, NZ = 4, 8
REST, CHUNK = 512, 256
BF16 = jnp.bfloat16
F32 = jnp.float32


def split(value):
    high = value.astype(BF16)
    return high, (value - high.astype(F32)).astype(BF16)


def swap(value):
    return lax.ppermute(value, "core", [(0, 1), (1, 0)])


def gather(value, axis):
    copies = jnp.broadcast_to(value[None], (lax.axis_size(axis),) + value.shape)
    return lax.all_to_all(copies, axis, 0, 0, tiled=True)


def shifts(value, axis):
    count = lax.axis_size(axis)
    sent = [lax.ppermute(value, axis, [(i, (i + step) % count) for i in range(count)]) for step in range(1, count)]
    return [value, *sent]


def first_kernel(
    own_x, own_screen, other_screen, coef_hbm, rest_0, rest_1, rest_2, rest_3, own_hbm, other_hbm, passed_hbm,
    out_hbm, passed_out_hbm, coef, rest, own, other, total, sums, coef_sem, rest_sem, own_sem, other_sem, out_sem,
):
    del passed_hbm, passed_out_hbm
    rests = rest_0, rest_1, rest_2, rest_3
    aux, full_depth, width = own.shape
    most = coef.shape[1]
    starts = [*range(0, most, CHUNK), most]
    ends = [*starts[1:], full_depth]

    def copies(step):
        rows = pl.ds(starts[step], ends[step] - starts[step])
        if starts[step] < most:
            columns = [pltpu.make_async_copy(coef_hbm.at[:, rows], coef.at[:, rows], coef_sem.at[step])]
        else:
            columns = [pltpu.make_async_copy(rests[x], rest.at[x], rest_sem.at[x]) for x in range(NX)]
        return (
            *columns,
            pltpu.make_async_copy(own_hbm.at[:, rows, :], own.at[:, rows, :], own_sem.at[step]),
            pltpu.make_async_copy(other_hbm.at[:, rows, :], other.at[:, rows, :], other_sem.at[step]),
        )

    def screened(integrals, screen, p, start, end):
        def tile(row, column):
            block = integrals[p, row * TILE : (row + 1) * TILE, column * TILE : (column + 1) * TILE]
            return block * screen[row, column].astype(F32)

        return jnp.concatenate(
            [
                jnp.concatenate([tile(row, column) for column in range(width // TILE)], axis=1)
                for row in range(start // TILE, end // TILE)
            ],
            axis=0,
        )

    for step in range(len(starts)):
        for copy in copies(step):
            copy.start()
    for step, (first_row, end_row) in enumerate(zip(starts, ends, strict=True)):
        for copy in copies(step):
            copy.wait()
        coef_high, coef_low = split(coef[:, first_row:end_row] if first_row < most else rest[...].reshape(-1, rest.shape[3]))
        for p in range(aux):
            for place, (integrals, screen) in enumerate(((own, own_screen), (other, other_screen))):
                high, low = split(screened(integrals, screen, p, first_row, end_row))
                part = jnp.dot(coef_high, low, preferred_element_type=F32)
                part += jnp.dot(coef_low, high, preferred_element_type=F32)
                part += jnp.dot(coef_high, high, preferred_element_type=F32)
                columns = slice((2 * p + place) * width, (2 * p + place + 1) * width)
                if step == 0:
                    total[:, columns] = part
                elif first_row < most:
                    total[:, columns] += part
                else:
                    for z in range(NZ):
                        for x in range(NX):
                            row = (x * NZ + z) * 16
                            true_x = lax.rem(own_x[0] + NX - x, NX)
                            start = pl.ds(pl.multiple_of((z * NX + true_x) * 16, 16), 16)
                            end = pl.ds(pl.multiple_of((true_x * NZ + z) * 16, 16), 16)
                            sums[end, columns] = total[start, columns] + part[row : row + 16]
    copy = pltpu.make_async_copy(sums, out_hbm, out_sem)
    copy.start()
    copy.wait()


def first(own_x, own_screen, other_screen, coef, rests, own, other, passed):
    occ, most = coef.shape
    aux, full_depth, half_width = own.shape
    steps = -(-most // CHUNK) + 1
    width = 2 * aux * half_width
    away, scalars = pl.BlockSpec(memory_space=pl.ANY), pl.BlockSpec(memory_space=pltpu.SMEM)
    sems = pltpu.SemaphoreType.DMA((steps,))
    return pl.pallas_call(
        first_kernel,
        out_shape=(
            jax.ShapeDtypeStruct((occ, width), F32),
            jax.ShapeDtypeStruct(passed.shape, passed.dtype),
        ),
        in_specs=[scalars] * 3 + [away] * (4 + NX),
        out_specs=(away, away),
        input_output_aliases={6 + NX: 1},
        scratch_shapes=[
            pltpu.VMEM(coef.shape, F32),
            pltpu.VMEM((NX, *rests[0].shape), F32),
            pltpu.VMEM(own.shape, F32),
            pltpu.VMEM(other.shape, F32),
            pltpu.VMEM((occ, width), F32),
            pltpu.VMEM((occ, width), F32),
            sems,
            pltpu.SemaphoreType.DMA((NX,)),
            sems,
            sems,
            pltpu.SemaphoreType.DMA,
        ],
        compiler_params=pltpu.CompilerParams(vmem_limit_bytes=56 * 2**20),
        cost_estimate=pl.CostEstimate(
            flops=6 * occ * full_depth * width, bytes_accessed=14 * 2**20, transcendentals=0
        ),
    )(own_x, own_screen, other_screen, coef, *rests, own, other, passed)


def second_kernel(rows_ref, halves_ref, out_ref):
    width = halves_ref.shape[2] // 4

    def nus(p, z, source):
        pair = halves_ref[source, z * 16 : z * 16 + 16, 2 * p * width : 2 * (p + 1) * width]
        return pair if source == 0 else jnp.concatenate([pair[:, width:], pair[:, :width]], axis=1)

    half = jnp.concatenate([nus(p, z, c) for p in range(2) for z in range(4) for c in range(2)], axis=0)
    half_high, half_low = split(half)
    rows_high, rows_low = split(rows_ref[...])

    def dot(a, b):
        return lax.dot_general(a, b, (((1,), (1,)), ((), ())), preferred_element_type=F32)

    out_ref[...] = (dot(rows_high, half_low) + dot(rows_low, half_high)) + dot(rows_high, half_high)


def second(rows, halves):
    vmem = pl.BlockSpec(memory_space=pltpu.VMEM)
    return pl.pallas_call(
        second_kernel,
        out_shape=jax.ShapeDtypeStruct((rows.shape[0], 4 * halves.shape[1]), F32),
        in_specs=[vmem, vmem],
        compiler_params=pltpu.CompilerParams(vmem_limit_bytes=32 * 2**20),
    )(rows, halves)


def last_kernel(parts_ref, out_ref):
    total = parts_ref[0]
    for place in range(1, parts_ref.shape[0]):
        total += parts_ref[place]
    width = out_ref.shape[2]
    for aux in range(2):
        out_ref[aux] = total[:, aux * width : (aux + 1) * width]


def last(parts):
    return pl.pallas_call(
        last_kernel,
        out_shape=jax.ShapeDtypeStruct((2, parts.shape[1], parts.shape[2] // 2), F32),
    )(parts)


def shards(integrals, coefs, screen, domains):
    aux, row_len, col_len = integrals.shape
    occ = coefs.shape[1]
    row = lax.axis_index("y")
    col = lax.axis_index(("x", "z", "core"))
    row_tiles = row_len // TILE

    tile_ids = row * row_tiles + jnp.arange(row_tiles, dtype=jnp.int32)
    listed = lax.dynamic_index_in_dim(domains, col * occ // TILE, 0, keepdims=False)
    in_domain = jnp.any(listed[None, :] == tile_ids[:, None], axis=1).astype(F32)
    coef = coefs.T * jnp.repeat(in_domain, TILE)[None, :]

    most = row_len - REST
    along_x = gather(coef[:, :most], "x")
    gathered = lax.all_gather(along_x.reshape(NX * occ, most), "z", axis=0, tiled=True)

    along_z = gather(coef[:, most:] + 0.0 * along_x[0, :, :REST], "z")
    rests = shifts(along_z, "x")

    along_y = gather(coef + 0.0 * jnp.pad(along_z[0], ((0, 0), (0, most))), "y")

    own_x = lax.axis_index("x")[None]
    half, along_y = first(own_x, screen, swap(screen), gathered, rests, integrals, swap(integrals), along_y)
    half = lax.psum_scatter(half, "y", scatter_dimension=0, tiled=True)

    chip_len = 2 * col_len
    along_y = along_y.reshape(8, occ, row_len // chip_len, chip_len).transpose(0, 2, 1, 3)
    rows = lax.all_to_all(along_y.reshape(NX * NZ, occ, chip_len), ("x", "z"), 0, 0, tiled=True)
    pairs = second(rows.reshape(NX * NZ * occ, chip_len), lax.all_gather(half, "core"))
    pairs = pairs.reshape(NX * NZ, occ, pairs.shape[1])
    pairs = lax.all_to_all(pairs, ("x", "z"), 0, 0, tiled=True)
    return last(pairs).transpose(0, 2, 1)


def solution(mesh):
    devices = mesh.devices.reshape(8, NX, NZ, 2)
    split_mesh = Mesh(devices, ("y", "x", "z", "core"))
    col = ("x", "z", "core")
    placed = (P(None, "y", col), P("y", col), P("y", col), P())
    return jax.shard_map(
        shards, mesh=split_mesh, in_specs=placed, out_specs=P(None, "y", col), check_vma=False
    )
```

```python
import jax
import jax.numpy as jnp
from jax import lax
from jax.experimental import pallas as pl
from jax.experimental.pallas import tpu as pltpu
from jax.sharding import Mesh, PartitionSpec as P

TILE = 128
NX, NZ = 4, 8
REST, CHUNK = 512, 256
BF16 = jnp.bfloat16
F32 = jnp.float32


def split(value):
    high = value.astype(BF16)
    return high, (value - high.astype(F32)).astype(BF16)


def swap(value):
    return lax.ppermute(value, "core", [(0, 1), (1, 0)])


def gather(value, axis):
    copies = jnp.broadcast_to(value[None], (lax.axis_size(axis),) + value.shape)
    return lax.all_to_all(copies, axis, 0, 0, tiled=True)


def shifts(value, axis):
    count = lax.axis_size(axis)
    sent = [lax.ppermute(value, axis, [(i, (i + step) % count) for i in range(count)]) for step in range(1, count)]
    return [value, *sent]


def first_kernel(
    own_x, own_screen, other_screen, coef_hbm, rest_0, rest_1, rest_2, rest_3, own_hbm, other_hbm, out_hbm,
    coef, rest, own, other, total, sums, coef_sem, rest_sem, own_sem, other_sem, out_sem,
):
    rests = rest_0, rest_1, rest_2, rest_3
    aux, full_depth, width = own.shape
    most = coef.shape[1]
    starts = [*range(0, most, CHUNK), most]
    ends = [*starts[1:], full_depth]

    def copies(step):
        rows = pl.ds(starts[step], ends[step] - starts[step])
        if starts[step] < most:
            columns = [pltpu.make_async_copy(coef_hbm.at[:, rows], coef.at[:, rows], coef_sem.at[step])]
        else:
            columns = [pltpu.make_async_copy(rests[x], rest.at[x], rest_sem.at[x]) for x in range(NX)]
        return (
            *columns,
            pltpu.make_async_copy(own_hbm.at[:, rows, :], own.at[:, rows, :], own_sem.at[step]),
            pltpu.make_async_copy(other_hbm.at[:, rows, :], other.at[:, rows, :], other_sem.at[step]),
        )

    def screened(integrals, screen, p, start, end):
        def tile(row, column):
            block = integrals[p, row * TILE : (row + 1) * TILE, column * TILE : (column + 1) * TILE]
            return block * screen[row, column].astype(F32)

        return jnp.concatenate(
            [
                jnp.concatenate([tile(row, column) for column in range(width // TILE)], axis=1)
                for row in range(start // TILE, end // TILE)
            ],
            axis=0,
        )

    for step in range(len(starts)):
        for copy in copies(step):
            copy.start()
    for step, (first_row, end_row) in enumerate(zip(starts, ends, strict=True)):
        for copy in copies(step):
            copy.wait()
        coef_high, coef_low = split(coef[:, first_row:end_row] if first_row < most else rest[...].reshape(-1, rest.shape[3]))
        for p in range(aux):
            for place, (integrals, screen) in enumerate(((own, own_screen), (other, other_screen))):
                high, low = split(screened(integrals, screen, p, first_row, end_row))
                part = jnp.dot(coef_high, low, preferred_element_type=F32)
                part += jnp.dot(coef_low, high, preferred_element_type=F32)
                part += jnp.dot(coef_high, high, preferred_element_type=F32)
                columns = slice((2 * p + place) * width, (2 * p + place + 1) * width)
                if step == 0:
                    total[:, columns] = part
                elif first_row < most:
                    total[:, columns] += part
                else:
                    for z in range(NZ):
                        for x in range(NX):
                            row = (x * NZ + z) * 16
                            true_x = lax.rem(own_x[0] + NX - x, NX)
                            start = pl.ds(pl.multiple_of((z * NX + true_x) * 16, 16), 16)
                            end = pl.ds(pl.multiple_of((true_x * NZ + z) * 16, 16), 16)
                            sums[end, columns] = total[start, columns] + part[row : row + 16]
    copy = pltpu.make_async_copy(sums, out_hbm, out_sem)
    copy.start()
    copy.wait()


def first(own_x, own_screen, other_screen, coef, rests, own, other):
    occ, most = coef.shape
    aux, full_depth, half_width = own.shape
    steps = -(-most // CHUNK) + 1
    width = 2 * aux * half_width
    away, scalars = pl.BlockSpec(memory_space=pl.ANY), pl.BlockSpec(memory_space=pltpu.SMEM)
    sems = pltpu.SemaphoreType.DMA((steps,))
    return pl.pallas_call(
        first_kernel,
        out_shape=jax.ShapeDtypeStruct((occ, width), F32),
        in_specs=[scalars] * 3 + [away] * (3 + NX),
        out_specs=away,
        scratch_shapes=[
            pltpu.VMEM(coef.shape, F32),
            pltpu.VMEM((NX, *rests[0].shape), F32),
            pltpu.VMEM(own.shape, F32),
            pltpu.VMEM(other.shape, F32),
            pltpu.VMEM((occ, width), F32),
            pltpu.VMEM((occ, width), F32),
            sems,
            pltpu.SemaphoreType.DMA((NX,)),
            sems,
            sems,
            pltpu.SemaphoreType.DMA,
        ],
        compiler_params=pltpu.CompilerParams(vmem_limit_bytes=56 * 2**20),
        cost_estimate=pl.CostEstimate(
            flops=6 * occ * full_depth * width, bytes_accessed=14 * 2**20, transcendentals=0
        ),
    )(own_x, own_screen, other_screen, coef, *rests, own, other)


def second_kernel(rows_ref, halves_ref, out_ref):
    width = halves_ref.shape[2] // 4

    def nus(p, z, source):
        pair = halves_ref[source, z * 16 : z * 16 + 16, 2 * p * width : 2 * (p + 1) * width]
        return pair if source == 0 else jnp.concatenate([pair[:, width:], pair[:, :width]], axis=1)

    half = jnp.concatenate([nus(p, z, c) for p in range(2) for z in range(4) for c in range(2)], axis=0)
    half_high, half_low = split(half)
    rows_high, rows_low = split(rows_ref[...])

    def dot(a, b):
        return lax.dot_general(a, b, (((1,), (1,)), ((), ())), preferred_element_type=F32)

    out_ref[...] = (dot(rows_high, half_low) + dot(rows_low, half_high)) + dot(rows_high, half_high)


def second(rows, halves):
    vmem = pl.BlockSpec(memory_space=pltpu.VMEM)
    return pl.pallas_call(
        second_kernel,
        out_shape=jax.ShapeDtypeStruct((rows.shape[0], 4 * halves.shape[1]), F32),
        in_specs=[vmem, vmem],
        compiler_params=pltpu.CompilerParams(vmem_limit_bytes=32 * 2**20),
    )(rows, halves)


def last_kernel(parts_ref, out_ref):
    total = parts_ref[0]
    for place in range(1, parts_ref.shape[0]):
        total += parts_ref[place]
    width = out_ref.shape[2]
    for aux in range(2):
        out_ref[aux] = total[:, aux * width : (aux + 1) * width]


def last(parts):
    return pl.pallas_call(
        last_kernel,
        out_shape=jax.ShapeDtypeStruct((2, parts.shape[1], parts.shape[2] // 2), F32),
    )(parts)


def shards(integrals, coefs, screen, domains):
    aux, row_len, col_len = integrals.shape
    occ = coefs.shape[1]
    row = lax.axis_index("y")
    col = lax.axis_index(("x", "z", "core"))
    row_tiles = row_len // TILE

    tile_ids = row * row_tiles + jnp.arange(row_tiles, dtype=jnp.int32)
    listed = lax.dynamic_index_in_dim(domains, col * occ // TILE, 0, keepdims=False)
    in_domain = jnp.any(listed[None, :] == tile_ids[:, None], axis=1).astype(F32)
    coef = coefs.T * jnp.repeat(in_domain, TILE)[None, :]

    most = row_len - REST
    along_x = gather(coef[:, :most], "x")
    gathered = lax.all_gather(along_x.reshape(NX * occ, most), "z", axis=0, tiled=True)

    along_z = gather(coef[:, most:] + 0.0 * along_x[0, :, :REST], "z")
    rests = shifts(along_z, "x")

    along_y = gather(coef + 0.0 * jnp.pad(along_z[0], ((0, 0), (0, most))), "y")

    own_x = lax.axis_index("x")[None]
    products = first(own_x, screen, swap(screen), gathered, rests, integrals, swap(integrals))
    half = lax.psum_scatter(products, "y", scatter_dimension=0, tiled=True)

    chip_len = 2 * col_len
    along_y = along_y.reshape(8, occ, row_len // chip_len, chip_len).transpose(0, 2, 1, 3)
    along_y = along_y.reshape(NX * NZ, occ, chip_len) + 0.0 * products[None, :occ, :chip_len]
    rows = lax.all_to_all(along_y, ("x", "z"), 0, 0, tiled=True)
    pairs = second(rows.reshape(NX * NZ * occ, chip_len), lax.all_gather(half, "core"))
    pairs = pairs.reshape(NX * NZ, occ, pairs.shape[1])
    pairs = lax.all_to_all(pairs, ("x", "z"), 0, 0, tiled=True)
    return last(pairs).transpose(0, 2, 1)


def solution(mesh):
    devices = mesh.devices.reshape(8, NX, NZ, 2)
    split_mesh = Mesh(devices, ("y", "x", "z", "core"))
    col = ("x", "z", "core")
    placed = (P(None, "y", col), P("y", col), P("y", col), P())
    return jax.shard_map(
        shards, mesh=split_mesh, in_specs=placed, out_specs=P(None, "y", col), check_vma=False
    )
```

```python
import jax
import jax.numpy as jnp
from jax import lax
from jax.experimental import pallas as pl
from jax.experimental.pallas import tpu as pltpu
from jax.sharding import Mesh, PartitionSpec as P

TILE = 128
NX, NZ = 4, 8
REST, CHUNK = 512, 256
BF16 = jnp.bfloat16
F32 = jnp.float32


def split(value):
    high = value.astype(BF16)
    return high, (value - high.astype(F32)).astype(BF16)


def swap(value):
    return lax.ppermute(value, "core", [(0, 1), (1, 0)])


def gather(value, axis):
    copies = jnp.broadcast_to(value[None], (lax.axis_size(axis),) + value.shape)
    return lax.all_to_all(copies, axis, 0, 0, tiled=True)


def shifts(value, axis):
    count = lax.axis_size(axis)
    sent = [lax.ppermute(value, axis, [(i, (i + step) % count) for i in range(count)]) for step in range(1, count)]
    return [value, *sent]


def first_kernel(
    own_x, own_screen, other_screen, coef_hbm, rest_0, rest_1, rest_2, rest_3, own_hbm, other_hbm, out_hbm,
    coef, rest, own, other, total, sums, coef_sem, rest_sem, own_sem, other_sem, out_sem,
):
    rests = rest_0, rest_1, rest_2, rest_3
    aux, full_depth, width = own.shape
    most = coef.shape[1]
    starts = [*range(0, most, CHUNK), most]
    ends = [*starts[1:], full_depth]

    def copies(step):
        rows = pl.ds(starts[step], ends[step] - starts[step])
        if starts[step] < most:
            columns = [pltpu.make_async_copy(coef_hbm.at[:, rows], coef.at[:, rows], coef_sem.at[step])]
        else:
            columns = [pltpu.make_async_copy(rests[x], rest.at[x], rest_sem.at[x]) for x in range(NX)]
        return (
            *columns,
            pltpu.make_async_copy(own_hbm.at[:, rows, :], own.at[:, rows, :], own_sem.at[step]),
            pltpu.make_async_copy(other_hbm.at[:, rows, :], other.at[:, rows, :], other_sem.at[step]),
        )

    def screened(integrals, screen, p, start, end):
        def tile(row, column):
            block = integrals[p, row * TILE : (row + 1) * TILE, column * TILE : (column + 1) * TILE]
            return block * screen[row, column].astype(F32)

        return jnp.concatenate(
            [
                jnp.concatenate([tile(row, column) for column in range(width // TILE)], axis=1)
                for row in range(start // TILE, end // TILE)
            ],
            axis=0,
        )

    for step in range(len(starts)):
        for copy in copies(step):
            copy.start()
    for step, (first_row, end_row) in enumerate(zip(starts, ends, strict=True)):
        for copy in copies(step):
            copy.wait()
        coef_high, coef_low = split(coef[:, first_row:end_row] if first_row < most else rest[...].reshape(-1, rest.shape[3]))
        for p in range(aux):
            for place, (integrals, screen) in enumerate(((own, own_screen), (other, other_screen))):
                high, low = split(screened(integrals, screen, p, first_row, end_row))
                part = jnp.dot(coef_high, low, preferred_element_type=F32)
                part += jnp.dot(coef_low, high, preferred_element_type=F32)
                part += jnp.dot(coef_high, high, preferred_element_type=F32)
                columns = slice((2 * p + place) * width, (2 * p + place + 1) * width)
                if step == 0:
                    total[:, columns] = part
                elif first_row < most:
                    total[:, columns] += part
                else:
                    for z in range(NZ):
                        for x in range(NX):
                            row = (x * NZ + z) * 16
                            true_x = lax.rem(own_x[0] + NX - x, NX)
                            start = pl.ds(pl.multiple_of((z * NX + true_x) * 16, 16), 16)
                            end = pl.ds(pl.multiple_of((true_x * NZ + z) * 16, 16), 16)
                            sums[end, columns] = total[start, columns] + part[row : row + 16]
    copy = pltpu.make_async_copy(sums, out_hbm, out_sem)
    copy.start()
    copy.wait()


def first(own_x, own_screen, other_screen, coef, rests, own, other):
    occ, most = coef.shape
    aux, full_depth, half_width = own.shape
    steps = -(-most // CHUNK) + 1
    width = 2 * aux * half_width
    away, scalars = pl.BlockSpec(memory_space=pl.ANY), pl.BlockSpec(memory_space=pltpu.SMEM)
    sems = pltpu.SemaphoreType.DMA((steps,))
    return pl.pallas_call(
        first_kernel,
        out_shape=jax.ShapeDtypeStruct((occ, width), F32),
        in_specs=[scalars] * 3 + [away] * (3 + NX),
        out_specs=away,
        scratch_shapes=[
            pltpu.VMEM(coef.shape, F32),
            pltpu.VMEM((NX, *rests[0].shape), F32),
            pltpu.VMEM(own.shape, F32),
            pltpu.VMEM(other.shape, F32),
            pltpu.VMEM((occ, width), F32),
            pltpu.VMEM((occ, width), F32),
            sems,
            pltpu.SemaphoreType.DMA((NX,)),
            sems,
            sems,
            pltpu.SemaphoreType.DMA,
        ],
        compiler_params=pltpu.CompilerParams(vmem_limit_bytes=56 * 2**20),
        cost_estimate=pl.CostEstimate(flops=0, bytes_accessed=0, transcendentals=0),
    )(own_x, own_screen, other_screen, coef, *rests, own, other)


def second_kernel(rows_ref, halves_ref, out_ref):
    width = halves_ref.shape[2] // 4

    def nus(p, z, source):
        pair = halves_ref[source, z * 16 : z * 16 + 16, 2 * p * width : 2 * (p + 1) * width]
        return pair if source == 0 else jnp.concatenate([pair[:, width:], pair[:, :width]], axis=1)

    half = jnp.concatenate([nus(p, z, c) for p in range(2) for z in range(4) for c in range(2)], axis=0)
    half_high, half_low = split(half)
    rows_high, rows_low = split(rows_ref[...])

    def dot(a, b):
        return lax.dot_general(a, b, (((1,), (1,)), ((), ())), preferred_element_type=F32)

    out_ref[...] = (dot(rows_high, half_low) + dot(rows_low, half_high)) + dot(rows_high, half_high)


def second(rows, halves):
    vmem = pl.BlockSpec(memory_space=pltpu.VMEM)
    return pl.pallas_call(
        second_kernel,
        out_shape=jax.ShapeDtypeStruct((rows.shape[0], 4 * halves.shape[1]), F32),
        in_specs=[vmem, vmem],
        compiler_params=pltpu.CompilerParams(vmem_limit_bytes=32 * 2**20),
    )(rows, halves)


def last_kernel(parts_ref, out_ref):
    total = parts_ref[0]
    for place in range(1, parts_ref.shape[0]):
        total += parts_ref[place]
    width = out_ref.shape[2]
    for aux in range(2):
        out_ref[aux] = total[:, aux * width : (aux + 1) * width]


def last(parts):
    return pl.pallas_call(
        last_kernel,
        out_shape=jax.ShapeDtypeStruct((2, parts.shape[1], parts.shape[2] // 2), F32),
    )(parts)


def shards(integrals, coefs, screen, domains):
    aux, row_len, col_len = integrals.shape
    occ = coefs.shape[1]
    row = lax.axis_index("y")
    col = lax.axis_index(("x", "z", "core"))
    row_tiles = row_len // TILE

    tile_ids = row * row_tiles + jnp.arange(row_tiles, dtype=jnp.int32)
    listed = lax.dynamic_index_in_dim(domains, col * occ // TILE, 0, keepdims=False)
    in_domain = jnp.any(listed[None, :] == tile_ids[:, None], axis=1).astype(F32)
    coef = coefs.T * jnp.repeat(in_domain, TILE)[None, :]

    most = row_len - REST
    along_x = gather(coef[:, :most], "x")
    gathered = lax.all_gather(along_x.reshape(NX * occ, most), "z", axis=0, tiled=True)

    along_z = gather(coef[:, most:] + 0.0 * along_x[0, :, :REST], "z")
    rests = shifts(along_z, "x")

    along_y = gather(coef + 0.0 * jnp.pad(along_z[0], ((0, 0), (0, most))), "y")

    own_x = lax.axis_index("x")[None]
    products = first(own_x, screen, swap(screen), gathered, rests, integrals, swap(integrals))
    half = lax.psum_scatter(products, "y", scatter_dimension=0, tiled=True)

    chip_len = 2 * col_len
    along_y = along_y.reshape(8, occ, row_len // chip_len, chip_len).transpose(0, 2, 1, 3)
    along_y = along_y.reshape(NX * NZ, occ, chip_len) + 0.0 * products[None, :occ, :chip_len]
    rows = lax.all_to_all(along_y, ("x", "z"), 0, 0, tiled=True)
    pairs = second(rows.reshape(NX * NZ * occ, chip_len), lax.all_gather(half, "core"))
    pairs = pairs.reshape(NX * NZ, occ, pairs.shape[1])
    pairs = lax.all_to_all(pairs, ("x", "z"), 0, 0, tiled=True)
    return last(pairs).transpose(0, 2, 1)


def solution(mesh):
    devices = mesh.devices.reshape(8, NX, NZ, 2)
    split_mesh = Mesh(devices, ("y", "x", "z", "core"))
    col = ("x", "z", "core")
    placed = (P(None, "y", col), P("y", col), P("y", col), P())
    return jax.shard_map(
        shards, mesh=split_mesh, in_specs=placed, out_specs=P(None, "y", col), check_vma=False
    )
```

```python
import jax
import jax.numpy as jnp
from jax import lax
from jax.experimental import pallas as pl
from jax.experimental.pallas import tpu as pltpu
from jax.sharding import Mesh, PartitionSpec as P

TILE = 128
NX, NZ = 4, 8
REST, CHUNK = 512, 256
BF16 = jnp.bfloat16
F32 = jnp.float32


def split(value):
    high = value.astype(BF16)
    return high, (value - high.astype(F32)).astype(BF16)


def swap(value):
    return lax.ppermute(value, "core", [(0, 1), (1, 0)])


def gather(value, axis):
    copies = jnp.broadcast_to(value[None], (lax.axis_size(axis),) + value.shape)
    return lax.all_to_all(copies, axis, 0, 0, tiled=True)


def shifts(value, axis):
    count = lax.axis_size(axis)
    sent = [lax.ppermute(value, axis, [(i, (i + step) % count) for i in range(count)]) for step in range(1, count)]
    return [value, *sent]


def first_kernel(
    own_x, own_screen, other_screen, coef_hbm, rest_0, rest_1, rest_2, rest_3, own_hbm, other_hbm, out_hbm,
    coef, rest, own, other, total, sums, coef_sem, rest_sem, own_sem, other_sem, out_sem,
):
    rests = rest_0, rest_1, rest_2, rest_3
    aux, full_depth, width = own.shape
    most = coef.shape[1]
    starts = [*range(0, most, CHUNK), most]
    ends = [*starts[1:], full_depth]

    def copies(step):
        rows = pl.ds(starts[step], ends[step] - starts[step])
        if starts[step] < most:
            columns = [pltpu.make_async_copy(coef_hbm.at[:, rows], coef.at[:, rows], coef_sem.at[step])]
        else:
            columns = [pltpu.make_async_copy(rests[x], rest.at[x], rest_sem.at[x]) for x in range(NX)]
        return (
            *columns,
            pltpu.make_async_copy(own_hbm.at[:, rows, :], own.at[:, rows, :], own_sem.at[step]),
            pltpu.make_async_copy(other_hbm.at[:, rows, :], other.at[:, rows, :], other_sem.at[step]),
        )

    def screened(integrals, screen, p, start, end):
        def tile(row, column):
            block = integrals[p, row * TILE : (row + 1) * TILE, column * TILE : (column + 1) * TILE]
            return block * screen[row, column].astype(F32)

        return jnp.concatenate(
            [
                jnp.concatenate([tile(row, column) for column in range(width // TILE)], axis=1)
                for row in range(start // TILE, end // TILE)
            ],
            axis=0,
        )

    for step in range(len(starts)):
        for copy in copies(step):
            copy.start()
    for step, (first_row, end_row) in enumerate(zip(starts, ends, strict=True)):
        for copy in copies(step):
            copy.wait()
        coef_high, coef_low = split(coef[:, first_row:end_row] if first_row < most else rest[...].reshape(-1, rest.shape[3]))
        for p in range(aux):
            for place, (integrals, screen) in enumerate(((own, own_screen), (other, other_screen))):
                high, low = split(screened(integrals, screen, p, first_row, end_row))
                part = jnp.dot(coef_high, low, preferred_element_type=F32)
                part += jnp.dot(coef_low, high, preferred_element_type=F32)
                part += jnp.dot(coef_high, high, preferred_element_type=F32)
                columns = slice((2 * p + place) * width, (2 * p + place + 1) * width)
                if step == 0:
                    total[:, columns] = part
                elif first_row < most:
                    total[:, columns] += part
                else:
                    for z in range(NZ):
                        for x in range(NX):
                            row = (x * NZ + z) * 16
                            true_x = lax.rem(own_x[0] + NX - x, NX)
                            start = pl.ds(pl.multiple_of((z * NX + true_x) * 16, 16), 16)
                            end = pl.ds(pl.multiple_of((true_x * NZ + z) * 16, 16), 16)
                            sums[end, columns] = total[start, columns] + part[row : row + 16]
    copy = pltpu.make_async_copy(sums, out_hbm, out_sem)
    copy.start()
    copy.wait()


def first(own_x, own_screen, other_screen, coef, rests, own, other):
    occ, most = coef.shape
    aux, full_depth, half_width = own.shape
    steps = -(-most // CHUNK) + 1
    width = 2 * aux * half_width
    away, scalars = pl.BlockSpec(memory_space=pl.ANY), pl.BlockSpec(memory_space=pltpu.SMEM)
    sems = pltpu.SemaphoreType.DMA((steps,))
    return pl.pallas_call(
        first_kernel,
        out_shape=jax.ShapeDtypeStruct((occ, width), F32),
        in_specs=[scalars] * 3 + [away] * (3 + NX),
        out_specs=away,
        scratch_shapes=[
            pltpu.VMEM(coef.shape, F32),
            pltpu.VMEM((NX, *rests[0].shape), F32),
            pltpu.VMEM(own.shape, F32),
            pltpu.VMEM(other.shape, F32),
            pltpu.VMEM((occ, width), F32),
            pltpu.VMEM((occ, width), F32),
            sems,
            pltpu.SemaphoreType.DMA((NX,)),
            sems,
            sems,
            pltpu.SemaphoreType.DMA,
        ],
        compiler_params=pltpu.CompilerParams(vmem_limit_bytes=56 * 2**20),
        cost_estimate=pl.CostEstimate(flops=0, bytes_accessed=0, transcendentals=0),
    )(own_x, own_screen, other_screen, coef, *rests, own, other)


def second_kernel(rows_ref, halves_ref, out_ref):
    width = halves_ref.shape[2] // 4

    def nus(p, z, source):
        pair = halves_ref[source, z * 16 : z * 16 + 16, 2 * p * width : 2 * (p + 1) * width]
        return pair if source == 0 else jnp.concatenate([pair[:, width:], pair[:, :width]], axis=1)

    half = jnp.concatenate([nus(p, z, c) for p in range(2) for z in range(4) for c in range(2)], axis=0)
    half_high, half_low = split(half)
    rows_high, rows_low = split(rows_ref[...])

    def dot(a, b):
        return lax.dot_general(a, b, (((1,), (1,)), ((), ())), preferred_element_type=F32)

    out_ref[...] = (dot(rows_high, half_low) + dot(rows_low, half_high)) + dot(rows_high, half_high)


def second(rows, halves):
    vmem = pl.BlockSpec(memory_space=pltpu.VMEM)
    return pl.pallas_call(
        second_kernel,
        out_shape=jax.ShapeDtypeStruct((rows.shape[0], 4 * halves.shape[1]), F32),
        in_specs=[vmem, vmem],
        compiler_params=pltpu.CompilerParams(vmem_limit_bytes=32 * 2**20),
    )(rows, halves)


def last_kernel(parts_ref, out_ref):
    total = parts_ref[0]
    for place in range(1, parts_ref.shape[0]):
        total += parts_ref[place]
    width = out_ref.shape[2]
    for aux in range(2):
        out_ref[aux] = total[:, aux * width : (aux + 1) * width]


def last(parts):
    return pl.pallas_call(
        last_kernel,
        out_shape=jax.ShapeDtypeStruct((2, parts.shape[1], parts.shape[2] // 2), F32),
    )(parts)


def shards(integrals, coefs, screen, domains):
    aux, row_len, col_len = integrals.shape
    occ = coefs.shape[1]
    row = lax.axis_index("y")
    col = lax.axis_index(("x", "z", "core"))
    row_tiles = row_len // TILE

    tile_ids = row * row_tiles + jnp.arange(row_tiles, dtype=jnp.int32)
    listed = lax.dynamic_index_in_dim(domains, col * occ // TILE, 0, keepdims=False)
    in_domain = jnp.any(listed[None, :] == tile_ids[:, None], axis=1).astype(F32)
    coef = coefs.T * jnp.repeat(in_domain, TILE)[None, :]

    most = row_len - REST
    along_x = gather(coef[:, :most], "x")
    gathered = lax.all_gather(along_x.reshape(NX * occ, most), "z", axis=0, tiled=True)

    along_z = gather(coef[:, most:] + 0.0 * along_x[0, :, :REST], "z")
    rests = shifts(along_z, "x")

    along_y = gather(coef + 0.0 * jnp.pad(along_x[0], ((0, 0), (0, REST))), "y")

    own_x = lax.axis_index("x")[None]
    products = first(own_x, screen, swap(screen), gathered, rests, integrals, swap(integrals))
    half = lax.psum_scatter(products, "y", scatter_dimension=0, tiled=True)

    chip_len = 2 * col_len
    along_y = along_y.reshape(8, occ, row_len // chip_len, chip_len).transpose(0, 2, 1, 3)
    along_y = along_y.reshape(NX * NZ, occ, chip_len) + 0.0 * products[None, :occ, :chip_len]
    rows = lax.all_to_all(along_y, ("x", "z"), 0, 0, tiled=True)
    pairs = second(rows.reshape(NX * NZ * occ, chip_len), lax.all_gather(half, "core"))
    pairs = pairs.reshape(NX * NZ, occ, pairs.shape[1])
    pairs = lax.all_to_all(pairs, ("x", "z"), 0, 0, tiled=True)
    return last(pairs).transpose(0, 2, 1)


def solution(mesh):
    devices = mesh.devices.reshape(8, NX, NZ, 2)
    split_mesh = Mesh(devices, ("y", "x", "z", "core"))
    col = ("x", "z", "core")
    placed = (P(None, "y", col), P("y", col), P("y", col), P())
    return jax.shard_map(
        shards, mesh=split_mesh, in_specs=placed, out_specs=P(None, "y", col), check_vma=False
    )
```

```python
import jax
import jax.numpy as jnp
from jax import lax
from jax.experimental import pallas as pl
from jax.experimental.pallas import tpu as pltpu
from jax.sharding import Mesh, PartitionSpec as P

TILE = 128
NX, NZ = 4, 8
REST, CHUNK = 512, 256
BF16 = jnp.bfloat16
F32 = jnp.float32


def split(value):
    high = value.astype(BF16)
    return high, (value - high.astype(F32)).astype(BF16)


def swap(value):
    return lax.ppermute(value, "core", [(0, 1), (1, 0)])


def gather(value, axis):
    copies = jnp.broadcast_to(value[None], (lax.axis_size(axis),) + value.shape)
    return lax.all_to_all(copies, axis, 0, 0, tiled=True)


def shifts(value, axis):
    count = lax.axis_size(axis)
    sent = [lax.ppermute(value, axis, [(i, (i + step) % count) for i in range(count)]) for step in range(1, count)]
    return [value, *sent]


def first_kernel(
    own_x, own_screen, other_screen, coef_hbm, rest_0, rest_1, rest_2, rest_3, own_hbm, other_hbm, out_hbm,
    coef, rest, own, other, total, sums, coef_sem, rest_sem, own_sem, other_sem, out_sem,
):
    rests = rest_0, rest_1, rest_2, rest_3
    aux, full_depth, width = own.shape
    most = coef.shape[1]
    starts = [*range(0, most, CHUNK), most]
    ends = [*starts[1:], full_depth]

    def copies(step):
        rows = pl.ds(starts[step], ends[step] - starts[step])
        if starts[step] < most:
            columns = [pltpu.make_async_copy(coef_hbm.at[:, rows], coef.at[:, rows], coef_sem.at[step])]
        else:
            columns = [pltpu.make_async_copy(rests[x], rest.at[x], rest_sem.at[x]) for x in range(NX)]
        return (
            *columns,
            pltpu.make_async_copy(own_hbm.at[:, rows, :], own.at[:, rows, :], own_sem.at[step]),
            pltpu.make_async_copy(other_hbm.at[:, rows, :], other.at[:, rows, :], other_sem.at[step]),
        )

    def screened(integrals, screen, p, start, end):
        def tile(row, column):
            block = integrals[p, row * TILE : (row + 1) * TILE, column * TILE : (column + 1) * TILE]
            return block * screen[row, column].astype(F32)

        return jnp.concatenate(
            [
                jnp.concatenate([tile(row, column) for column in range(width // TILE)], axis=1)
                for row in range(start // TILE, end // TILE)
            ],
            axis=0,
        )

    for step in range(len(starts)):
        for copy in copies(step):
            copy.start()
    outs = []
    for step, (first_row, end_row) in enumerate(zip(starts, ends, strict=True)):
        for copy in copies(step):
            copy.wait()
        coef_high, coef_low = split(coef[:, first_row:end_row] if first_row < most else rest[...].reshape(-1, rest.shape[3]))
        for p in range(aux):
            for place, (integrals, screen) in enumerate(((own, own_screen), (other, other_screen))):
                high, low = split(screened(integrals, screen, p, first_row, end_row))
                part = jnp.dot(coef_high, low, preferred_element_type=F32)
                part += jnp.dot(coef_low, high, preferred_element_type=F32)
                part += jnp.dot(coef_high, high, preferred_element_type=F32)
                columns = slice((2 * p + place) * width, (2 * p + place + 1) * width)
                if step == 0:
                    total[:, columns] = part
                elif first_row < most:
                    total[:, columns] += part
                else:
                    for z in range(NZ):
                        for x in range(NX):
                            row = (x * NZ + z) * 16
                            true_x = lax.rem(own_x[0] + NX - x, NX)
                            start = pl.ds(pl.multiple_of((z * NX + true_x) * 16, 16), 16)
                            end = pl.ds(pl.multiple_of((true_x * NZ + z) * 16, 16), 16)
                            sums[end, columns] = total[start, columns] + part[row : row + 16]
                    block = 2 * p + place
                    outs.append(pltpu.make_async_copy(sums.at[:, columns], out_hbm.at[:, columns], out_sem.at[block]))
                    outs[-1].start()
    for copy in outs:
        copy.wait()


def first(own_x, own_screen, other_screen, coef, rests, own, other):
    occ, most = coef.shape
    aux, full_depth, half_width = own.shape
    steps = -(-most // CHUNK) + 1
    width = 2 * aux * half_width
    away, scalars = pl.BlockSpec(memory_space=pl.ANY), pl.BlockSpec(memory_space=pltpu.SMEM)
    sems = pltpu.SemaphoreType.DMA((steps,))
    return pl.pallas_call(
        first_kernel,
        out_shape=jax.ShapeDtypeStruct((occ, width), F32),
        in_specs=[scalars] * 3 + [away] * (3 + NX),
        out_specs=away,
        scratch_shapes=[
            pltpu.VMEM(coef.shape, F32),
            pltpu.VMEM((NX, *rests[0].shape), F32),
            pltpu.VMEM(own.shape, F32),
            pltpu.VMEM(other.shape, F32),
            pltpu.VMEM((occ, width), F32),
            pltpu.VMEM((occ, width), F32),
            sems,
            pltpu.SemaphoreType.DMA((NX,)),
            sems,
            sems,
            pltpu.SemaphoreType.DMA((2 * aux,)),
        ],
        compiler_params=pltpu.CompilerParams(vmem_limit_bytes=56 * 2**20),
        cost_estimate=pl.CostEstimate(flops=0, bytes_accessed=0, transcendentals=0),
    )(own_x, own_screen, other_screen, coef, *rests, own, other)


def second_kernel(rows_ref, halves_ref, out_ref):
    width = halves_ref.shape[2] // 4

    def nus(p, z, source):
        pair = halves_ref[source, z * 16 : z * 16 + 16, 2 * p * width : 2 * (p + 1) * width]
        return pair if source == 0 else jnp.concatenate([pair[:, width:], pair[:, :width]], axis=1)

    half = jnp.concatenate([nus(p, z, c) for p in range(2) for z in range(4) for c in range(2)], axis=0)
    half_high, half_low = split(half)
    rows_high, rows_low = split(rows_ref[...])

    def dot(a, b):
        return lax.dot_general(a, b, (((1,), (1,)), ((), ())), preferred_element_type=F32)

    out_ref[...] = (dot(rows_high, half_low) + dot(rows_low, half_high)) + dot(rows_high, half_high)


def second(rows, halves):
    vmem = pl.BlockSpec(memory_space=pltpu.VMEM)
    return pl.pallas_call(
        second_kernel,
        out_shape=jax.ShapeDtypeStruct((rows.shape[0], 4 * halves.shape[1]), F32),
        in_specs=[vmem, vmem],
        compiler_params=pltpu.CompilerParams(vmem_limit_bytes=32 * 2**20),
    )(rows, halves)


def last_kernel(parts_ref, out_ref):
    total = parts_ref[0]
    for place in range(1, parts_ref.shape[0]):
        total += parts_ref[place]
    width = out_ref.shape[2]
    for aux in range(2):
        out_ref[aux] = total[:, aux * width : (aux + 1) * width]


def last(parts):
    return pl.pallas_call(
        last_kernel,
        out_shape=jax.ShapeDtypeStruct((2, parts.shape[1], parts.shape[2] // 2), F32),
    )(parts)


def shards(integrals, coefs, screen, domains):
    aux, row_len, col_len = integrals.shape
    occ = coefs.shape[1]
    row = lax.axis_index("y")
    col = lax.axis_index(("x", "z", "core"))
    row_tiles = row_len // TILE

    tile_ids = row * row_tiles + jnp.arange(row_tiles, dtype=jnp.int32)
    listed = lax.dynamic_index_in_dim(domains, col * occ // TILE, 0, keepdims=False)
    in_domain = jnp.any(listed[None, :] == tile_ids[:, None], axis=1).astype(F32)
    coef = coefs.T * jnp.repeat(in_domain, TILE)[None, :]

    most = row_len - REST
    along_x = gather(coef[:, :most], "x")
    gathered = lax.all_gather(along_x.reshape(NX * occ, most), "z", axis=0, tiled=True)

    along_z = gather(coef[:, most:], "z")
    rests = shifts(along_z, "x")

    along_y = gather(coef + 0.0 * jnp.pad(along_z[0], ((0, 0), (0, most))), "y")

    own_x = lax.axis_index("x")[None]
    products = first(own_x, screen, swap(screen), gathered, rests, integrals, swap(integrals))
    half = lax.psum_scatter(products, "y", scatter_dimension=0, tiled=True)

    chip_len = 2 * col_len
    along_y = along_y.reshape(8, occ, row_len // chip_len, chip_len).transpose(0, 2, 1, 3)
    along_y = along_y.reshape(NX * NZ, occ, chip_len) + 0.0 * products[None, :occ, :chip_len]
    rows = lax.all_to_all(along_y, ("x", "z"), 0, 0, tiled=True)
    pairs = second(rows.reshape(NX * NZ * occ, chip_len), lax.all_gather(half, "core"))
    pairs = pairs.reshape(NX * NZ, occ, pairs.shape[1])
    pairs = lax.all_to_all(pairs, ("x", "z"), 0, 0, tiled=True)
    return last(pairs).transpose(0, 2, 1)


def solution(mesh):
    devices = mesh.devices.reshape(8, NX, NZ, 2)
    split_mesh = Mesh(devices, ("y", "x", "z", "core"))
    col = ("x", "z", "core")
    placed = (P(None, "y", col), P("y", col), P("y", col), P())
    return jax.shard_map(
        shards, mesh=split_mesh, in_specs=placed, out_specs=P(None, "y", col), check_vma=False
    )
```

```python
import jax
import jax.numpy as jnp
from jax import lax
from jax.experimental import pallas as pl
from jax.experimental.pallas import tpu as pltpu
from jax.sharding import Mesh, PartitionSpec as P

TILE = 128
NX, NZ = 4, 8
REST, CHUNK = 512, 256
BF16 = jnp.bfloat16
F32 = jnp.float32


def split(value):
    high = value.astype(BF16)
    return high, (value - high.astype(F32)).astype(BF16)


def swap(value):
    return lax.ppermute(value, "core", [(0, 1), (1, 0)])


def gather(value, axis):
    copies = jnp.broadcast_to(value[None], (lax.axis_size(axis),) + value.shape)
    return lax.all_to_all(copies, axis, 0, 0, tiled=True)


def shifts(value, axis):
    count = lax.axis_size(axis)
    sent = [lax.ppermute(value, axis, [(i, (i + step) % count) for i in range(count)]) for step in range(1, count)]
    return [value, *sent]


def first_kernel(
    own_x, own_screen, other_screen, coef_hbm, rest_0, rest_1, rest_2, rest_3, own_hbm, other_hbm, out_hbm,
    coef, rest, own, other, total, sums, coef_sem, rest_sem, own_sem, other_sem, out_sem,
):
    rests = rest_0, rest_1, rest_2, rest_3
    aux, full_depth, width = own.shape
    most = coef.shape[1]
    starts = [*range(0, most, CHUNK), most]
    ends = [*starts[1:], full_depth]

    def copies(step):
        rows = pl.ds(starts[step], ends[step] - starts[step])
        if starts[step] < most:
            columns = [pltpu.make_async_copy(coef_hbm.at[:, rows], coef.at[:, rows], coef_sem.at[step])]
        else:
            columns = [pltpu.make_async_copy(rests[x], rest.at[x], rest_sem.at[x]) for x in range(NX)]
        return (
            *columns,
            pltpu.make_async_copy(own_hbm.at[:, rows, :], own.at[:, rows, :], own_sem.at[step]),
            pltpu.make_async_copy(other_hbm.at[:, rows, :], other.at[:, rows, :], other_sem.at[step]),
        )

    def screened(integrals, screen, p, start, end):
        def tile(row, column):
            block = integrals[p, row * TILE : (row + 1) * TILE, column * TILE : (column + 1) * TILE]
            return block * screen[row, column].astype(F32)

        return jnp.concatenate(
            [
                jnp.concatenate([tile(row, column) for column in range(width // TILE)], axis=1)
                for row in range(start // TILE, end // TILE)
            ],
            axis=0,
        )

    for step in range(len(starts)):
        for copy in copies(step):
            copy.start()
    outs = []
    for step, (first_row, end_row) in enumerate(zip(starts, ends, strict=True)):
        for copy in copies(step):
            copy.wait()
        coef_high, coef_low = split(coef[:, first_row:end_row] if first_row < most else rest[...].reshape(-1, rest.shape[3]))
        for p in range(aux):
            for place, (integrals, screen) in enumerate(((own, own_screen), (other, other_screen))):
                high, low = split(screened(integrals, screen, p, first_row, end_row))
                part = jnp.dot(coef_high, low, preferred_element_type=F32)
                part += jnp.dot(coef_low, high, preferred_element_type=F32)
                part += jnp.dot(coef_high, high, preferred_element_type=F32)
                columns = slice((2 * p + place) * width, (2 * p + place + 1) * width)
                if step == 0:
                    total[:, columns] = part
                elif first_row < most:
                    total[:, columns] += part
                else:
                    for z in range(NZ):
                        for x in range(NX):
                            row = (x * NZ + z) * 16
                            true_x = lax.rem(own_x[0] + NX - x, NX)
                            start = pl.ds(pl.multiple_of((z * NX + true_x) * 16, 16), 16)
                            end = pl.ds(pl.multiple_of((true_x * NZ + z) * 16, 16), 16)
                            sums[end, columns] = total[start, columns] + part[row : row + 16]
                    block = 2 * p + place
                    outs.append(pltpu.make_async_copy(sums.at[:, columns], out_hbm.at[:, columns], out_sem.at[block]))
                    outs[-1].start()
    for copy in outs:
        copy.wait()


def first(own_x, own_screen, other_screen, coef, rests, own, other):
    occ, most = coef.shape
    aux, full_depth, half_width = own.shape
    steps = -(-most // CHUNK) + 1
    width = 2 * aux * half_width
    away, scalars = pl.BlockSpec(memory_space=pl.ANY), pl.BlockSpec(memory_space=pltpu.SMEM)
    sems = pltpu.SemaphoreType.DMA((steps,))
    return pl.pallas_call(
        first_kernel,
        out_shape=jax.ShapeDtypeStruct((occ, width), F32),
        in_specs=[scalars] * 3 + [away] * (3 + NX),
        out_specs=away,
        scratch_shapes=[
            pltpu.VMEM(coef.shape, F32),
            pltpu.VMEM((NX, *rests[0].shape), F32),
            pltpu.VMEM(own.shape, F32),
            pltpu.VMEM(other.shape, F32),
            pltpu.VMEM((occ, width), F32),
            pltpu.VMEM((occ, width), F32),
            sems,
            pltpu.SemaphoreType.DMA((NX,)),
            sems,
            sems,
            pltpu.SemaphoreType.DMA((2 * aux,)),
        ],
        compiler_params=pltpu.CompilerParams(vmem_limit_bytes=56 * 2**20),
        cost_estimate=pl.CostEstimate(flops=0, bytes_accessed=0, transcendentals=0),
    )(own_x, own_screen, other_screen, coef, *rests, own, other)


def second_kernel(rows_ref, halves_ref, out_ref):
    width = halves_ref.shape[2] // 4

    def nus(p, z, source):
        pair = halves_ref[source, z * 16 : z * 16 + 16, 2 * p * width : 2 * (p + 1) * width]
        return pair if source == 0 else jnp.concatenate([pair[:, width:], pair[:, :width]], axis=1)

    half = jnp.concatenate([nus(p, z, c) for p in range(2) for z in range(4) for c in range(2)], axis=0)
    half_high, half_low = split(half)
    rows_high, rows_low = split(rows_ref[...])

    def dot(a, b):
        return lax.dot_general(a, b, (((1,), (1,)), ((), ())), preferred_element_type=F32)

    out_ref[...] = (dot(rows_high, half_low) + dot(rows_low, half_high)) + dot(rows_high, half_high)


def second(rows, halves):
    vmem = pl.BlockSpec(memory_space=pltpu.VMEM)
    return pl.pallas_call(
        second_kernel,
        out_shape=jax.ShapeDtypeStruct((rows.shape[0], 4 * halves.shape[1]), F32),
        in_specs=[vmem, vmem],
        compiler_params=pltpu.CompilerParams(vmem_limit_bytes=32 * 2**20),
    )(rows, halves)


def last_kernel(parts_ref, out_ref):
    total = parts_ref[0]
    for place in range(1, parts_ref.shape[0]):
        total += parts_ref[place]
    width = out_ref.shape[2]
    for aux in range(2):
        out_ref[aux] = total[:, aux * width : (aux + 1) * width]


def last(parts):
    return pl.pallas_call(
        last_kernel,
        out_shape=jax.ShapeDtypeStruct((2, parts.shape[1], parts.shape[2] // 2), F32),
        in_specs=[pl.BlockSpec(memory_space=pltpu.VMEM)],
        compiler_params=pltpu.CompilerParams(vmem_limit_bytes=8 * 2**20),
    )(parts)


def shards(integrals, coefs, screen, domains):
    aux, row_len, col_len = integrals.shape
    occ = coefs.shape[1]
    row = lax.axis_index("y")
    col = lax.axis_index(("x", "z", "core"))
    row_tiles = row_len // TILE

    tile_ids = row * row_tiles + jnp.arange(row_tiles, dtype=jnp.int32)
    listed = lax.dynamic_index_in_dim(domains, col * occ // TILE, 0, keepdims=False)
    in_domain = jnp.any(listed[None, :] == tile_ids[:, None], axis=1).astype(F32)
    coef = coefs.T * jnp.repeat(in_domain, TILE)[None, :]

    most = row_len - REST
    along_x = gather(coef[:, :most], "x")
    gathered = lax.all_gather(along_x.reshape(NX * occ, most), "z", axis=0, tiled=True)

    along_z = gather(coef[:, most:], "z")
    rests = shifts(along_z, "x")

    along_y = gather(coef + 0.0 * jnp.pad(along_z[0], ((0, 0), (0, most))), "y")

    own_x = lax.axis_index("x")[None]
    products = first(own_x, screen, swap(screen), gathered, rests, integrals, swap(integrals))
    half = lax.psum_scatter(products, "y", scatter_dimension=0, tiled=True)

    chip_len = 2 * col_len
    along_y = along_y.reshape(8, occ, row_len // chip_len, chip_len).transpose(0, 2, 1, 3)
    along_y = along_y.reshape(NX * NZ, occ, chip_len) + 0.0 * products[None, :occ, :chip_len]
    rows = lax.all_to_all(along_y, ("x", "z"), 0, 0, tiled=True)
    pairs = second(rows.reshape(NX * NZ * occ, chip_len), lax.all_gather(half, "core"))
    pairs = pairs.reshape(NX * NZ, occ, pairs.shape[1])
    pairs = lax.all_to_all(pairs, ("x", "z"), 0, 0, tiled=True)
    return last(pairs).transpose(0, 2, 1)


def solution(mesh):
    devices = mesh.devices.reshape(8, NX, NZ, 2)
    split_mesh = Mesh(devices, ("y", "x", "z", "core"))
    col = ("x", "z", "core")
    placed = (P(None, "y", col), P("y", col), P("y", col), P())
    return jax.shard_map(
        shards, mesh=split_mesh, in_specs=placed, out_specs=P(None, "y", col), check_vma=False
    )
```

```python
import jax
import jax.numpy as jnp
from jax import lax
from jax.experimental import pallas as pl
from jax.experimental.pallas import tpu as pltpu
from jax.sharding import Mesh, PartitionSpec as P

TILE = 128
NX, NZ = 4, 8
REST = 512
STARTS = 0, 256, 768
BF16 = jnp.bfloat16
F32 = jnp.float32


def split(value):
    high = value.astype(BF16)
    return high, (value - high.astype(F32)).astype(BF16)


def swap(value):
    return lax.ppermute(value, "core", [(0, 1), (1, 0)])


def gather(value, axis):
    copies = jnp.broadcast_to(value[None], (lax.axis_size(axis),) + value.shape)
    return lax.all_to_all(copies, axis, 0, 0, tiled=True)


def shifts(value, axis):
    count = lax.axis_size(axis)
    sent = [lax.ppermute(value, axis, [(i, (i + step) % count) for i in range(count)]) for step in range(1, count)]
    return [value, *sent]


def first_kernel(
    own_x, own_screen, other_screen, coef_hbm, rest_0, rest_1, rest_2, rest_3, own_hbm, other_hbm, out_hbm,
    coef, rest, own, other, total, sums, coef_sem, rest_sem, own_sem, other_sem, out_sem,
):
    rests = rest_0, rest_1, rest_2, rest_3
    aux, full_depth, width = own.shape
    most = coef.shape[1]
    starts = [*STARTS, most]
    ends = [*starts[1:], full_depth]

    def copies(step):
        rows = pl.ds(starts[step], ends[step] - starts[step])
        if starts[step] < most:
            columns = [pltpu.make_async_copy(coef_hbm.at[:, rows], coef.at[:, rows], coef_sem.at[step])]
        else:
            columns = [pltpu.make_async_copy(rests[x], rest.at[x], rest_sem.at[x]) for x in range(NX)]
        return (
            *columns,
            pltpu.make_async_copy(own_hbm.at[:, rows, :], own.at[:, rows, :], own_sem.at[step]),
            pltpu.make_async_copy(other_hbm.at[:, rows, :], other.at[:, rows, :], other_sem.at[step]),
        )

    def screened(integrals, screen, p, start, end):
        def tile(row, column):
            block = integrals[p, row * TILE : (row + 1) * TILE, column * TILE : (column + 1) * TILE]
            return block * screen[row, column].astype(F32)

        return jnp.concatenate(
            [
                jnp.concatenate([tile(row, column) for column in range(width // TILE)], axis=1)
                for row in range(start // TILE, end // TILE)
            ],
            axis=0,
        )

    for step in range(len(starts)):
        for copy in copies(step):
            copy.start()
    outs = []
    for step, (first_row, end_row) in enumerate(zip(starts, ends, strict=True)):
        for copy in copies(step):
            copy.wait()
        coef_high, coef_low = split(coef[:, first_row:end_row] if first_row < most else rest[...].reshape(-1, rest.shape[3]))
        for p in range(aux):
            for place, (integrals, screen) in enumerate(((own, own_screen), (other, other_screen))):
                high, low = split(screened(integrals, screen, p, first_row, end_row))
                part = jnp.dot(coef_high, low, preferred_element_type=F32)
                part += jnp.dot(coef_low, high, preferred_element_type=F32)
                part += jnp.dot(coef_high, high, preferred_element_type=F32)
                columns = slice((2 * p + place) * width, (2 * p + place + 1) * width)
                if step == 0:
                    total[:, columns] = part
                elif first_row < most:
                    total[:, columns] += part
                else:
                    for z in range(NZ):
                        for x in range(NX):
                            row = (x * NZ + z) * 16
                            true_x = lax.rem(own_x[0] + NX - x, NX)
                            start = pl.ds(pl.multiple_of((z * NX + true_x) * 16, 16), 16)
                            end = pl.ds(pl.multiple_of((true_x * NZ + z) * 16, 16), 16)
                            sums[end, columns] = total[start, columns] + part[row : row + 16]
                    block = 2 * p + place
                    outs.append(pltpu.make_async_copy(sums.at[:, columns], out_hbm.at[:, columns], out_sem.at[block]))
                    outs[-1].start()
    for copy in outs:
        copy.wait()


def first(own_x, own_screen, other_screen, coef, rests, own, other):
    occ, most = coef.shape
    aux, full_depth, half_width = own.shape
    steps = len(STARTS) + 1
    width = 2 * aux * half_width
    away, scalars = pl.BlockSpec(memory_space=pl.ANY), pl.BlockSpec(memory_space=pltpu.SMEM)
    sems = pltpu.SemaphoreType.DMA((steps,))
    return pl.pallas_call(
        first_kernel,
        out_shape=jax.ShapeDtypeStruct((occ, width), F32),
        in_specs=[scalars] * 3 + [away] * (3 + NX),
        out_specs=away,
        scratch_shapes=[
            pltpu.VMEM(coef.shape, F32),
            pltpu.VMEM((NX, *rests[0].shape), F32),
            pltpu.VMEM(own.shape, F32),
            pltpu.VMEM(other.shape, F32),
            pltpu.VMEM((occ, width), F32),
            pltpu.VMEM((occ, width), F32),
            sems,
            pltpu.SemaphoreType.DMA((NX,)),
            sems,
            sems,
            pltpu.SemaphoreType.DMA((2 * aux,)),
        ],
        compiler_params=pltpu.CompilerParams(vmem_limit_bytes=56 * 2**20),
        cost_estimate=pl.CostEstimate(flops=0, bytes_accessed=0, transcendentals=0),
    )(own_x, own_screen, other_screen, coef, *rests, own, other)


def second_kernel(rows_ref, halves_ref, out_ref):
    width = halves_ref.shape[2] // 4

    def nus(p, z, source):
        pair = halves_ref[source, z * 16 : z * 16 + 16, 2 * p * width : 2 * (p + 1) * width]
        return pair if source == 0 else jnp.concatenate([pair[:, width:], pair[:, :width]], axis=1)

    half = jnp.concatenate([nus(p, z, c) for p in range(2) for z in range(4) for c in range(2)], axis=0)
    half_high, half_low = split(half)
    rows_high, rows_low = split(rows_ref[...])

    def dot(a, b):
        return lax.dot_general(a, b, (((1,), (1,)), ((), ())), preferred_element_type=F32)

    out_ref[...] = (dot(rows_high, half_low) + dot(rows_low, half_high)) + dot(rows_high, half_high)


def second(rows, halves):
    vmem = pl.BlockSpec(memory_space=pltpu.VMEM)
    return pl.pallas_call(
        second_kernel,
        out_shape=jax.ShapeDtypeStruct((rows.shape[0], 4 * halves.shape[1]), F32),
        in_specs=[vmem, vmem],
        compiler_params=pltpu.CompilerParams(vmem_limit_bytes=32 * 2**20),
    )(rows, halves)


def last_kernel(parts_ref, out_ref):
    total = parts_ref[0]
    for place in range(1, parts_ref.shape[0]):
        total += parts_ref[place]
    width = out_ref.shape[2]
    for aux in range(2):
        out_ref[aux] = total[:, aux * width : (aux + 1) * width]


def last(parts):
    return pl.pallas_call(
        last_kernel,
        out_shape=jax.ShapeDtypeStruct((2, parts.shape[1], parts.shape[2] // 2), F32),
        in_specs=[pl.BlockSpec(memory_space=pltpu.VMEM)],
        compiler_params=pltpu.CompilerParams(vmem_limit_bytes=8 * 2**20),
    )(parts)


def shards(integrals, coefs, screen, domains):
    aux, row_len, col_len = integrals.shape
    occ = coefs.shape[1]
    row = lax.axis_index("y")
    col = lax.axis_index(("x", "z", "core"))
    row_tiles = row_len // TILE

    tile_ids = row * row_tiles + jnp.arange(row_tiles, dtype=jnp.int32)
    listed = lax.dynamic_index_in_dim(domains, col * occ // TILE, 0, keepdims=False)
    in_domain = jnp.any(listed[None, :] == tile_ids[:, None], axis=1).astype(F32)
    coef = coefs.T * jnp.repeat(in_domain, TILE)[None, :]

    most = row_len - REST
    along_x = gather(coef[:, :most], "x")
    gathered = lax.all_gather(along_x.reshape(NX * occ, most), "z", axis=0, tiled=True)

    along_z = gather(coef[:, most:], "z")
    rests = shifts(along_z, "x")

    along_y = gather(coef + 0.0 * jnp.pad(along_z[0], ((0, 0), (0, most))), "y")

    own_x = lax.axis_index("x")[None]
    products = first(own_x, screen, swap(screen), gathered, rests, integrals, swap(integrals))
    half = lax.psum_scatter(products, "y", scatter_dimension=0, tiled=True)

    chip_len = 2 * col_len
    along_y = along_y.reshape(8, occ, row_len // chip_len, chip_len).transpose(0, 2, 1, 3)
    along_y = along_y.reshape(NX * NZ, occ, chip_len) + 0.0 * products[None, :occ, :chip_len]
    rows = lax.all_to_all(along_y, ("x", "z"), 0, 0, tiled=True)
    pairs = second(rows.reshape(NX * NZ * occ, chip_len), lax.all_gather(half, "core"))
    pairs = pairs.reshape(NX * NZ, occ, pairs.shape[1])
    pairs = lax.all_to_all(pairs, ("x", "z"), 0, 0, tiled=True)
    return last(pairs).transpose(0, 2, 1)


def solution(mesh):
    devices = mesh.devices.reshape(8, NX, NZ, 2)
    split_mesh = Mesh(devices, ("y", "x", "z", "core"))
    col = ("x", "z", "core")
    placed = (P(None, "y", col), P("y", col), P("y", col), P())
    return jax.shard_map(
        shards, mesh=split_mesh, in_specs=placed, out_specs=P(None, "y", col), check_vma=False
    )
```

```python
import jax
import jax.numpy as jnp
from jax import lax
from jax.experimental import pallas as pl
from jax.experimental.pallas import tpu as pltpu
from jax.sharding import Mesh, PartitionSpec as P

TILE = 128
NX, NZ = 4, 8
REST = 384
STARTS = 0, 256, 768
BF16 = jnp.bfloat16
F32 = jnp.float32


def split(value):
    high = value.astype(BF16)
    return high, (value - high.astype(F32)).astype(BF16)


def swap(value):
    return lax.ppermute(value, "core", [(0, 1), (1, 0)])


def gather(value, axis):
    copies = jnp.broadcast_to(value[None], (lax.axis_size(axis),) + value.shape)
    return lax.all_to_all(copies, axis, 0, 0, tiled=True)


def shifts(value, axis):
    count = lax.axis_size(axis)
    sent = [lax.ppermute(value, axis, [(i, (i + step) % count) for i in range(count)]) for step in range(1, count)]
    return [value, *sent]


def first_kernel(
    own_x, own_screen, other_screen, coef_hbm, rest_0, rest_1, rest_2, rest_3, own_hbm, other_hbm, out_hbm,
    coef, rest, own, other, total, sums, coef_sem, rest_sem, own_sem, other_sem, out_sem,
):
    rests = rest_0, rest_1, rest_2, rest_3
    aux, full_depth, width = own.shape
    most = coef.shape[1]
    starts = [*STARTS, most]
    ends = [*starts[1:], full_depth]

    def copies(step):
        rows = pl.ds(starts[step], ends[step] - starts[step])
        if starts[step] < most:
            columns = [pltpu.make_async_copy(coef_hbm.at[:, rows], coef.at[:, rows], coef_sem.at[step])]
        else:
            columns = [pltpu.make_async_copy(rests[x], rest.at[x], rest_sem.at[x]) for x in range(NX)]
        return (
            *columns,
            pltpu.make_async_copy(own_hbm.at[:, rows, :], own.at[:, rows, :], own_sem.at[step]),
            pltpu.make_async_copy(other_hbm.at[:, rows, :], other.at[:, rows, :], other_sem.at[step]),
        )

    def screened(integrals, screen, p, start, end):
        def tile(row, column):
            block = integrals[p, row * TILE : (row + 1) * TILE, column * TILE : (column + 1) * TILE]
            return block * screen[row, column].astype(F32)

        return jnp.concatenate(
            [
                jnp.concatenate([tile(row, column) for column in range(width // TILE)], axis=1)
                for row in range(start // TILE, end // TILE)
            ],
            axis=0,
        )

    for step in range(len(starts)):
        for copy in copies(step):
            copy.start()
    outs = []
    for step, (first_row, end_row) in enumerate(zip(starts, ends, strict=True)):
        for copy in copies(step):
            copy.wait()
        coef_high, coef_low = split(coef[:, first_row:end_row] if first_row < most else rest[...].reshape(-1, rest.shape[3]))
        for p in range(aux):
            for place, (integrals, screen) in enumerate(((own, own_screen), (other, other_screen))):
                high, low = split(screened(integrals, screen, p, first_row, end_row))
                part = jnp.dot(coef_high, low, preferred_element_type=F32)
                part += jnp.dot(coef_low, high, preferred_element_type=F32)
                part += jnp.dot(coef_high, high, preferred_element_type=F32)
                columns = slice((2 * p + place) * width, (2 * p + place + 1) * width)
                if step == 0:
                    total[:, columns] = part
                elif first_row < most:
                    total[:, columns] += part
                else:
                    for z in range(NZ):
                        for x in range(NX):
                            row = (x * NZ + z) * 16
                            true_x = lax.rem(own_x[0] + NX - x, NX)
                            start = pl.ds(pl.multiple_of((z * NX + true_x) * 16, 16), 16)
                            end = pl.ds(pl.multiple_of((true_x * NZ + z) * 16, 16), 16)
                            sums[end, columns] = total[start, columns] + part[row : row + 16]
                    block = 2 * p + place
                    outs.append(pltpu.make_async_copy(sums.at[:, columns], out_hbm.at[:, columns], out_sem.at[block]))
                    outs[-1].start()
    for copy in outs:
        copy.wait()


def first(own_x, own_screen, other_screen, coef, rests, own, other):
    occ, most = coef.shape
    aux, full_depth, half_width = own.shape
    steps = len(STARTS) + 1
    width = 2 * aux * half_width
    away, scalars = pl.BlockSpec(memory_space=pl.ANY), pl.BlockSpec(memory_space=pltpu.SMEM)
    sems = pltpu.SemaphoreType.DMA((steps,))
    return pl.pallas_call(
        first_kernel,
        out_shape=jax.ShapeDtypeStruct((occ, width), F32),
        in_specs=[scalars] * 3 + [away] * (3 + NX),
        out_specs=away,
        scratch_shapes=[
            pltpu.VMEM(coef.shape, F32),
            pltpu.VMEM((NX, *rests[0].shape), F32),
            pltpu.VMEM(own.shape, F32),
            pltpu.VMEM(other.shape, F32),
            pltpu.VMEM((occ, width), F32),
            pltpu.VMEM((occ, width), F32),
            sems,
            pltpu.SemaphoreType.DMA((NX,)),
            sems,
            sems,
            pltpu.SemaphoreType.DMA((2 * aux,)),
        ],
        compiler_params=pltpu.CompilerParams(vmem_limit_bytes=56 * 2**20),
        cost_estimate=pl.CostEstimate(flops=0, bytes_accessed=0, transcendentals=0),
    )(own_x, own_screen, other_screen, coef, *rests, own, other)


def second_kernel(rows_ref, halves_ref, out_ref):
    width = halves_ref.shape[2] // 4

    def nus(p, z, source):
        pair = halves_ref[source, z * 16 : z * 16 + 16, 2 * p * width : 2 * (p + 1) * width]
        return pair if source == 0 else jnp.concatenate([pair[:, width:], pair[:, :width]], axis=1)

    half = jnp.concatenate([nus(p, z, c) for p in range(2) for z in range(4) for c in range(2)], axis=0)
    half_high, half_low = split(half)
    rows_high, rows_low = split(rows_ref[...])

    def dot(a, b):
        return lax.dot_general(a, b, (((1,), (1,)), ((), ())), preferred_element_type=F32)

    out_ref[...] = (dot(rows_high, half_low) + dot(rows_low, half_high)) + dot(rows_high, half_high)


def second(rows, halves):
    vmem = pl.BlockSpec(memory_space=pltpu.VMEM)
    return pl.pallas_call(
        second_kernel,
        out_shape=jax.ShapeDtypeStruct((rows.shape[0], 4 * halves.shape[1]), F32),
        in_specs=[vmem, vmem],
        compiler_params=pltpu.CompilerParams(vmem_limit_bytes=32 * 2**20),
    )(rows, halves)


def last_kernel(parts_ref, out_ref):
    total = parts_ref[0]
    for place in range(1, parts_ref.shape[0]):
        total += parts_ref[place]
    width = out_ref.shape[2]
    for aux in range(2):
        out_ref[aux] = total[:, aux * width : (aux + 1) * width]


def last(parts):
    return pl.pallas_call(
        last_kernel,
        out_shape=jax.ShapeDtypeStruct((2, parts.shape[1], parts.shape[2] // 2), F32),
        in_specs=[pl.BlockSpec(memory_space=pltpu.VMEM)],
        compiler_params=pltpu.CompilerParams(vmem_limit_bytes=8 * 2**20),
    )(parts)


def shards(integrals, coefs, screen, domains):
    aux, row_len, col_len = integrals.shape
    occ = coefs.shape[1]
    row = lax.axis_index("y")
    col = lax.axis_index(("x", "z", "core"))
    row_tiles = row_len // TILE

    tile_ids = row * row_tiles + jnp.arange(row_tiles, dtype=jnp.int32)
    listed = lax.dynamic_index_in_dim(domains, col * occ // TILE, 0, keepdims=False)
    in_domain = jnp.any(listed[None, :] == tile_ids[:, None], axis=1).astype(F32)
    coef = coefs.T * jnp.repeat(in_domain, TILE)[None, :]

    most = row_len - REST
    along_x = gather(coef[:, :most], "x")
    gathered = lax.all_gather(along_x.reshape(NX * occ, most), "z", axis=0, tiled=True)

    along_z = gather(coef[:, most:], "z")
    rests = shifts(along_z, "x")

    along_y = gather(coef + 0.0 * jnp.pad(along_z[0], ((0, 0), (0, most))), "y")

    own_x = lax.axis_index("x")[None]
    products = first(own_x, screen, swap(screen), gathered, rests, integrals, swap(integrals))
    half = lax.psum_scatter(products, "y", scatter_dimension=0, tiled=True)

    chip_len = 2 * col_len
    along_y = along_y.reshape(8, occ, row_len // chip_len, chip_len).transpose(0, 2, 1, 3)
    along_y = along_y.reshape(NX * NZ, occ, chip_len) + 0.0 * products[None, :occ, :chip_len]
    rows = lax.all_to_all(along_y, ("x", "z"), 0, 0, tiled=True)
    pairs = second(rows.reshape(NX * NZ * occ, chip_len), lax.all_gather(half, "core"))
    pairs = pairs.reshape(NX * NZ, occ, pairs.shape[1])
    pairs = lax.all_to_all(pairs, ("x", "z"), 0, 0, tiled=True)
    return last(pairs).transpose(0, 2, 1)


def solution(mesh):
    devices = mesh.devices.reshape(8, NX, NZ, 2)
    split_mesh = Mesh(devices, ("y", "x", "z", "core"))
    col = ("x", "z", "core")
    placed = (P(None, "y", col), P("y", col), P("y", col), P())
    return jax.shard_map(
        shards, mesh=split_mesh, in_specs=placed, out_specs=P(None, "y", col), check_vma=False
    )
```
